1024 devices in a mesh: slab: 64 (over x, z), layer: 16 (over y, core).
Axes of the slice: x: 8, y: 8, z: 8, core: 2. Of those that a mesh axis runs over, the one named last changes fastest.
Arguments:
- adjoint_source: float32 [16, 1024, 4096], P('layer', 'slab')
- conductivity: float32 [16, 1024, 4096], P('layer', 'slab'), may hold values from 0.3 to 3
- tile_owner: int32 [8, 32], replicated, may hold values from 0 to 63, as said below
Outputs:
- adjoint: float32 [16, 1024, 4096], P('layer', 'slab')
- owned_grad: float32 [256, 128, 128], P('slab', 'layer')
The draws below stay inside these ranges and needn't reach their ends.
Inputs may be any that keep to these rules, and one draw needn't show every extreme that they name: `tile_owner`: every owner holds exactly 4 tiles, and in every row of tiles each owner holds at most 1 tile; in every row some owner holds 1 tile.
All inputs are finite; a program needn't handle non-finite values.
Results may differ from the reference program's by a relative error of at most 0.0003.
Values sent between devices are 32-bit elements; how exact they have to be, the bound alone decides.
No kernel may reach another device: no remote copies, remote signals or barrier semaphores. Data moves between devices by JAX's collectives and lax.ppermute only.
A program may use at most 32 MiB of HBM per device.

```python
import math
import jax
import jax.numpy as jnp

TILE = 128
TC = 32
ITERS = 3
NX = 1024
NY = 4096
NL = 16
TR = 8
N_SLAB = 64


def draw_adjoint_source(key, part):
    key = jax.random.fold_in(key, 11)
    layer_pos = jnp.arange(NL, dtype=jnp.float32)[:, None, None] / max(NL - 1, 1)
    row_pos = jnp.arange(NX, dtype=jnp.float32)[None, :, None] / max(NX - 1, 1)
    rough = jax.random.normal(key, (NL, NX, NY), jnp.float32)
    growth = jnp.power(3.0, row_pos) * jnp.power(3.0, layer_pos)
    return (growth * rough).astype(jnp.float32)


def draw_tile_owner(key, part):
    key = jax.random.fold_in(key, 23)
    first_key, second_key = jax.random.split(key)
    relabel = jax.random.permutation(first_key, N_SLAB)

    def shuffle_row(row_key):
        return jax.random.permutation(row_key, TC)
    columns = jax.vmap(shuffle_row)(jax.random.split(second_key, TR))
    position = (jnp.arange(TR, dtype=jnp.int32)[:, None] * TC + columns.astype(jnp.int32)) % N_SLAB
    return relabel[position].astype(jnp.int32)


def block_scale(rng, extent, shards, least, top_value):
    loudness = 1.0
    for dim, blocks in shards:
        heights = jax.random.uniform(jax.random.fold_in(jax.random.fold_in(rng, 6), dim), (blocks,), jnp.float32, least / len(shards), top_value / len(shards))
        loudness = loudness * jnp.repeat(jnp.exp(heights), extent[dim] // blocks).reshape((-1,) + (1,) * (len(extent) - 1 - dim))
    return loudness


def setup_inputs(seed: int = 0) -> dict:
    seeds = jax.random.split(jax.random.key(seed), 4)
    adjoint_source = draw_adjoint_source(jax.random.fold_in(seeds[3], 71), 0)
    conductivity = jnp.clip(jnp.exp(math.log(3.0) - 2.3025851 * jax.random.uniform(seeds[1], (NL, NX, NY), jnp.float32) ** block_scale(seeds[1], (NL, NX, NY), ((0, 16), (1, 64)), -0.2, 0.2)), 0.3, 3.0)
    tile_owner = draw_tile_owner(jax.random.fold_in(seeds[3], 71), 0)
    return {"adjoint_source": adjoint_source, "conductivity": conductivity, "tile_owner": tile_owner}


def neighbours(padded):
    return [padded[2:, 1:-1, 1:-1], padded[:-2, 1:-1, 1:-1],
            padded[1:-1, 2:, 1:-1], padded[1:-1, :-2, 1:-1],
            padded[1:-1, 1:-1, 2:], padded[1:-1, 1:-1, :-2]]


def apply_operator(field, conductivity):
    result = jnp.zeros_like(field)
    cond_near = neighbours(jnp.pad(conductivity, 1))
    field_near = neighbours(jnp.pad(field, 1))
    for near_cond, near_field in zip(cond_near, field_near):
        result = result + 0.5 * (conductivity + near_cond) * (field - near_field)
    return result


def reference(adjoint_source, conductivity, tile_owner):
    diagonal = jnp.zeros_like(conductivity)
    for near_cond in neighbours(jnp.pad(conductivity, 1)):
        diagonal = diagonal + 0.5 * (conductivity + near_cond)
    inverse = 1.0 / diagonal
    solution = jnp.zeros_like(adjoint_source)
    residual = adjoint_source
    precond = inverse * residual
    direction = precond
    inner_now = jnp.sum(residual * precond)
    for iteration in range(ITERS):
        product_field = apply_operator(direction, conductivity)
        step_size = inner_now / jnp.sum(direction * product_field)
        solution = solution + step_size * direction
        residual = residual - step_size * product_field
        if iteration + 1 < ITERS:
            precond = inverse * residual
            inner_next = jnp.sum(residual * precond)
            direction = precond + (inner_next / inner_now) * direction
            inner_now = inner_next
    gradient = jnp.sum(solution, axis=0)
    tile_blocks = gradient.reshape(TR, TILE, TC, TILE).transpose(0, 2, 3, 1).reshape(TR * TC, TILE, TILE)
    tile_order = jnp.argsort(tile_owner.reshape(-1), stable=True)
    return solution, tile_blocks[tile_order]
```

```python
import jax
import jax.numpy as jnp
from jax import lax
from jax.experimental import pallas as pl
from jax.experimental.pallas import tpu as pltpu
from jax.sharding import PartitionSpec as P

F32 = jnp.float32
LAYERS = 16
ROWS = 16
COLS = 4096
WIDTH = COLS // LAYERS
SLABS = 64
TILE_COLS = 32
PER_TILE = 8
OWNED = 4
EXT_ROWS = 24
EXT_COLS = 384
VMEM_LIMIT = 48 * 1024 * 1024


def lanes():
    return lax.broadcasted_iota(jnp.int32, (8, 128), 1)


def sublanes():
    return lax.broadcasted_iota(jnp.int32, (8, 128), 0)


def pack_kernel(cond_ref, src_ref, out_ref):
    lane = lanes()
    zero = jnp.zeros((8, 128), F32)
    for j in range(LAYERS):
        edge = zero
        for q, ref in enumerate((cond_ref, src_ref)):
            for g in range(2):
                rows = slice(8 * g, 8 * g + 8)
                base = WIDTH * j
                for t in range(2):
                    out_ref[j, 4 * q + 2 * g + t] = ref[0, rows, base + 128 * t : base + 128 * t + 128]
                before = ref[0, rows, base - 128 : base] if j > 0 else zero
                after = ref[0, rows, base + 256 : base + 384] if j < LAYERS - 1 else zero
                both = jnp.where(lane < 4, after, jnp.where(lane >= 124, before, 0.0))
                edge = edge + pltpu.roll(both, 4 + 8 * (2 * q + g), axis=1)
        out_ref[j, 8] = edge


def halo_kernel(recv_ref, up_ref, down_ref):
    sub = sublanes()
    for l in range(LAYERS):
        for t in range(2):
            up_ref[l, t] = jnp.where(sub >= 4, recv_ref[l, 2 + t], pltpu.roll(recv_ref[l, 6 + t], 4, axis=0))
            down_ref[l, t] = jnp.where(sub < 4, recv_ref[l, t], pltpu.roll(recv_ref[l, 4 + t], 4, axis=0))
        edge = recv_ref[l, 8]
        up_ref[l, 2] = edge
        down_ref[l, 2] = edge


def own(value):
    return value[:ROWS, :WIDTH]


def folded(value):
    return (value[:8, :128] + value[8:, :128]) + (value[:8, 128:] + value[8:, 128:])


def krylov_kernel(
    recv_ref, low_ref, high_ref, msg_ref, ret_ref, k_ref, v0_ref, v1_ref, v2_ref, inv_ref, cc_ref, cr_ref, cz_ref, square_ref
):
    lane = lanes()
    sub = sublanes()
    rim = (lane < 4) | (lane >= 124)
    blank = jnp.zeros((EXT_ROWS, EXT_COLS), F32)
    for ref in (k_ref, v0_ref, v1_ref, v2_ref):
        ref[LAYERS] = blank

    def spread(tile, index):
        return jnp.where(rim, pltpu.roll(tile, 128 - (4 + 8 * index), axis=1), 0.0)

    def unpack(l, _):
        edge = recv_ref[l, 8]
        high_edge = high_ref[l, 2]
        low_edge = pltpu.roll(low_ref[l, 2], 120, axis=1)
        halo_edge = jnp.where(sub < 4, high_edge, low_edge)
        for q, ref in enumerate((k_ref, v0_ref)):
            for g in range(2):
                for t in range(2):
                    ref[l, 8 * g : 8 * g + 8, 128 * t : 128 * t + 128] = recv_ref[l, 4 * q + 2 * g + t]
                ref[l, 8 * g : 8 * g + 8, 256:384] = spread(edge, 2 * q + g)
            ref[l, 16:24, 256:384] = spread(halo_edge, 2 * q)
        for t in range(2):
            cols = slice(128 * t, 128 * t + 128)
            high = high_ref[l, t]
            low = low_ref[l, t]
            k_ref[l, 16:24, cols] = jnp.where(sub < 4, high, low)
            v0_ref[l, 16:24, cols] = pltpu.roll(jnp.where(sub < 4, low, high), 4, axis=0)
        return 0

    lax.fori_loop(0, LAYERS, unpack, 0)

    def setup(l, carry):
        cz_before, s0, m0 = carry
        k = k_ref[l]
        cc = k + pltpu.roll(k, EXT_COLS - 1, axis=1)
        cr = k + pltpu.roll(k, EXT_ROWS - 1, axis=0)
        cz = k + k_ref[l + 1]
        diag = (cc + pltpu.roll(cc, 1, axis=1)) + (cr + pltpu.roll(cr, 1, axis=0)) + (cz + cz_before)
        inv = jnp.where(k > 0.0, 1.0 / diag, 0.0)
        twice = v0_ref[l] * 2.0
        v0 = twice * inv
        cc_ref[l] = cc
        cr_ref[l] = cr
        cz_ref[l] = cz
        inv_ref[l] = inv
        v0_ref[l] = v0
        mine = own(v0)
        for g in range(2):
            for t in range(2):
                ret_ref[l, 2 * g + t] = mine[8 * g : 8 * g + 8, 128 * t : 128 * t + 128]
        return cz, s0 + folded(mine * own(twice)), m0 + mine

    none = jnp.zeros((8, 128), F32)
    no_map = jnp.zeros((ROWS, WIDTH), F32)
    _, s0, m0 = lax.fori_loop(0, LAYERS, setup, (k_ref[0], none, no_map))

    def image(l, v_ref, fz_before):
        v = v_ref[l]
        fc = cc_ref[l] * (v - pltpu.roll(v, EXT_COLS - 1, axis=1))
        fr = cr_ref[l] * (v - pltpu.roll(v, EXT_ROWS - 1, axis=0))
        fz = cz_ref[l] * (v - v_ref[l + 1])
        result = (fc - pltpu.roll(fc, 1, axis=1)) + (fr - pltpu.roll(fr, 1, axis=0)) + (fz - fz_before)
        return v, result, fz

    def step(v_ref, out_ref, slot):
        def body(l, carry):
            fz_before, odd, even, total = carry
            v, result, fz = image(l, v_ref, fz_before)
            after = inv_ref[l] * result
            out_ref[l] = after
            mine = own(after)
            for g in range(2):
                for t in range(2):
                    ret_ref[l, 4 * slot + 2 * g + t] = mine[8 * g : 8 * g + 8, 128 * t : 128 * t + 128]
            got = own(result)
            return fz, odd + folded(own(v) * got), even + folded(mine * got), total + mine

        start = (-(k_ref[0] * v_ref[0]), none, none, no_map)
        return lax.fori_loop(0, LAYERS, body, start)[1:]

    s1, s2, m1 = step(v0_ref, v1_ref, 1)
    s3, s4, m2 = step(v1_ref, v2_ref, 2)

    def last(l, carry):
        fz_before, odd = carry
        v, result, fz = image(l, v2_ref, fz_before)
        return fz, odd + folded(own(v) * own(result))

    _, s5 = lax.fori_loop(0, LAYERS, last, (-(k_ref[0] * v2_ref[0]), none))

    sums = none
    for n, part in enumerate((s0, s1, s2, s3, s4, s5)):
        sums = jnp.where(sub == n, jnp.sum(part), sums)
    for t in range(2):
        for f, total in enumerate((m0, m1, m2)):
            square_ref[48 * t + 16 * f : 48 * t + 16 * f + 16, :] = total[:, 128 * t : 128 * t + 128]
    square_ref[96:104, :] = sums
    square_ref[104:128, :] = jnp.zeros((24, 128), F32)
    turned = square_ref[...].T
    for j in range(LAYERS):
        msg_ref[j] = turned[8 * j : 8 * j + 8, :]


def tree(values):
    while len(values) > 1:
        values = [a + b for a, b in zip(values[::2], values[1::2])]
    return values[0]


def route_kernel(owner_ref, index_ref, recv_ref, msg_ref):
    lane = lanes()
    total = tree([recv_ref[j] for j in range(LAYERS)])
    common = pltpu.roll(total, 80, axis=1)
    for o in range(SLABS):
        msg_ref[o] = common
    row = index_ref[0] // PER_TILE
    for c in range(TILE_COLS):
        strip = recv_ref[c // 2]
        if c % 2:
            strip = pltpu.roll(strip, 80, axis=1)
        msg_ref[owner_ref[row, c]] = jnp.where(lane < 48, strip, common)


def weights(s):
    s0, s1, s2, s3, s4, s5 = s
    a0 = s0 / s1
    z1 = -a0
    n1 = s0 + z1 * (2.0 * s1 + z1 * s2)
    b0 = n1 / s0
    p0, p1 = 1.0 + b0, z1
    a1 = n1 / (p0 * p0 * s1 + p1 * (2.0 * p0 * s2 + p1 * s3))
    x0, x1 = a0 + a1 * p0, a1 * p1
    z1, z2 = z1 - a1 * p0, -(a1 * p1)
    n2 = s0 + z1 * (2.0 * s1 + z1 * s2) + z2 * (2.0 * (s2 + z1 * s3) + z2 * s4)
    b1 = n2 / n1
    p0, p1, p2 = 1.0 + b1 * p0, z1 + b1 * p1, z2
    energy = p0 * p0 * s1 + p1 * (2.0 * p0 * s2 + p1 * s3) + p2 * (2.0 * (p0 * s3 + p1 * s4) + p2 * s5)
    a2 = n2 / energy
    return x0 + a2 * p0, x1 + a2 * p1, a2 * p2


def finish_kernel(rows_ref, recv_ref, ret_ref, adjoint_ref, owned_ref):
    lane = lanes()
    total = tree([recv_ref[s] for s in range(SLABS)])
    moments = [jnp.broadcast_to(total[:, 48 + n : 49 + n], (8, 128)) for n in range(6)]
    w0, w1, w2 = weights(moments)
    for j in range(LAYERS):
        for g in range(2):
            for t in range(2):
                n = 2 * g + t
                value = w0 * ret_ref[j, n] + w1 * ret_ref[j, 4 + n] + w2 * ret_ref[j, 8 + n]
                col = WIDTH * j + 128 * t
                adjoint_ref[0, 8 * g : 8 * g + 8, col : col + 128] = value
    for k in range(OWNED):
        row = rows_ref[k]
        tile = jnp.zeros((8, 128), F32)
        for i in range(PER_TILE):
            strip = recv_ref[PER_TILE * row + i]
            value = w0 * strip + w1 * pltpu.roll(strip, 112, axis=1) + w2 * pltpu.roll(strip, 96, axis=1)
            if i:
                value = pltpu.roll(value, 16 * i, axis=1)
            tile = jnp.where((lane >= 16 * i) & (lane < 16 * i + 16), value, tile)
        owned_ref[k] = tile


VMEM = pl.BlockSpec(memory_space=pltpu.VMEM)
SMEM = pl.BlockSpec(memory_space=pltpu.SMEM)


def shape(*dims):
    return jax.ShapeDtypeStruct(dims, F32)


def call(kernel, ins, outs, scratch=(), interpret=False):
    single = len(outs) == 1
    return pl.pallas_call(
        kernel,
        out_shape=outs[0] if single else tuple(outs),
        in_specs=ins,
        out_specs=VMEM if single else tuple(VMEM for _ in outs),
        scratch_shapes=list(scratch),
        compiler_params=pltpu.CompilerParams(vmem_limit_bytes=VMEM_LIMIT),
        interpret=interpret,
    )


def pack(cond, src, interpret=False):
    return call(pack_kernel, [VMEM] * 2, [shape(LAYERS, 9, 8, 128)], interpret=interpret)(cond, src)


def halo(recv, interpret=False):
    side = shape(LAYERS, 3, 8, 128)
    return call(halo_kernel, [VMEM], [side, side], interpret=interpret)(recv)


def krylov(recv, low, high, interpret=False):
    field = pltpu.VMEM((LAYERS + 1, EXT_ROWS, EXT_COLS), F32)
    face = pltpu.VMEM((LAYERS, EXT_ROWS, EXT_COLS), F32)
    return call(
        krylov_kernel,
        [VMEM] * 3,
        [shape(LAYERS, 8, 128), shape(LAYERS, 12, 8, 128)],
        [field] * 4 + [face] * 4 + [pltpu.VMEM((128, 128), F32)],
        interpret=interpret,
    )(recv, low, high)


def route(owner, index, recv, interpret=False):
    return call(route_kernel, [SMEM, SMEM, VMEM], [shape(SLABS, 8, 128)], interpret=interpret)(owner, index, recv)


def finish(rows, recv, ret, interpret=False):
    return call(
        finish_kernel, [SMEM, VMEM, VMEM], [shape(1, ROWS, COLS), shape(OWNED, 8, 128)], interpret=interpret
    )(rows, recv, ret)


def owned_rows(tile_owner, index):
    held = jnp.any(tile_owner == index, axis=1)
    rank = jnp.cumsum(held.astype(jnp.int32)) - 1
    slot = jnp.arange(OWNED, dtype=jnp.int32)[:, None]
    row = jnp.arange(tile_owner.shape[0], dtype=jnp.int32)[None, :]
    return jnp.sum(jnp.where(held[None, :] & (rank[None, :] == slot), row, 0), axis=1)


def per_device(adjoint_source, conductivity, tile_owner):
    index = lax.axis_index("slab")
    count = lax.axis_size("slab")
    recv = lax.all_to_all(pack(conductivity, adjoint_source), "layer", 0, 0, tiled=True)
    up, down = halo(recv)
    low = lax.ppermute(up, "slab", [(i, i + 1) for i in range(count - 1)])
    high = lax.ppermute(down, "slab", [(i + 1, i) for i in range(count - 1)])
    msg, ret = krylov(recv, low, high)
    strips = lax.all_to_all(msg, "layer", 0, 0, tiled=True)
    back = lax.all_to_all(ret, "layer", 0, 0, tiled=True)
    outgoing = route(tile_owner, index.reshape(1), strips)
    received = lax.all_to_all(outgoing, "slab", 0, 0, tiled=True)
    return finish(owned_rows(tile_owner, index), received, back)


def solution(mesh):
    placed = (P("layer", "slab", None), P("layer", "slab", None), P())
    return jax.shard_map(
        per_device,
        mesh=mesh,
        in_specs=placed,
        out_specs=(P("layer", "slab", None), P("slab", "layer", None)),
        check_vma=False,
    )
```

```python
import jax
import jax.numpy as jnp
from jax import lax
from jax.experimental import pallas as pl
from jax.experimental.pallas import tpu as pltpu
from jax.sharding import PartitionSpec as P

F32 = jnp.float32
LAYERS = 16
ROWS = 16
COLS = 4096
WIDTH = COLS // LAYERS
SLABS = 64
TILE_COLS = 32
PER_TILE = 8
OWNED = 4
EXT_ROWS = 24
EXT_COLS = 384
VMEM_LIMIT = 48 * 1024 * 1024


def lanes():
    return lax.broadcasted_iota(jnp.int32, (8, 128), 1)


def sublanes():
    return lax.broadcasted_iota(jnp.int32, (8, 128), 0)


def pack_kernel(cond_ref, src_ref, out_ref):
    lane = lanes()
    zero = jnp.zeros((8, 128), F32)
    for j in range(LAYERS):
        edge = zero
        for q, ref in enumerate((cond_ref, src_ref)):
            for g in range(2):
                rows = slice(8 * g, 8 * g + 8)
                base = WIDTH * j
                for t in range(2):
                    out_ref[j, 4 * q + 2 * g + t] = ref[0, rows, base + 128 * t : base + 128 * t + 128]
                before = ref[0, rows, base - 128 : base] if j > 0 else zero
                after = ref[0, rows, base + 256 : base + 384] if j < LAYERS - 1 else zero
                both = jnp.where(lane < 4, after, jnp.where(lane >= 124, before, 0.0))
                edge = edge + pltpu.roll(both, 4 + 8 * (2 * g + q), axis=1)
        out_ref[j, 8] = edge


def halo_kernel(recv_ref, up_ref, down_ref):
    lane = lanes()
    sub = sublanes()
    up_edges = [jnp.zeros((8, 128), F32)] * 2
    down_edges = [jnp.zeros((8, 128), F32)] * 2
    for l in range(LAYERS):
        for t in range(2):
            up_ref[2 * l + t] = jnp.where(sub >= 4, recv_ref[l, 2 + t], pltpu.roll(recv_ref[l, 6 + t], 4, axis=0))
            down_ref[2 * l + t] = jnp.where(sub < 4, recv_ref[l, t], pltpu.roll(recv_ref[l, 4 + t], 4, axis=0))
        edge = recv_ref[l, 8]
        half, place = l // 8, 16 * (l % 8)
        here = (lane >= place) & (lane < place + 16)
        up_edges[half] = jnp.where(here, pltpu.roll(edge, (place + 112) % 128, axis=1), up_edges[half])
        down_edges[half] = jnp.where(here, pltpu.roll(edge, place, axis=1), down_edges[half])
    up_ref[32] = jnp.where(sub >= 4, up_edges[0], pltpu.roll(up_edges[1], 4, axis=0))
    down_ref[32] = jnp.where(sub < 4, down_edges[0], pltpu.roll(down_edges[1], 4, axis=0))


def own(value):
    return value[:ROWS, :WIDTH]


def folded(value):
    return (value[:8, :128] + value[8:, :128]) + (value[:8, 128:] + value[8:, 128:])


def krylov_kernel(
    recv_ref, low_ref, high_ref, ret_ref, k_ref, v0_ref, v1_ref, v2_ref, inv_ref, cc_ref, cr_ref, cz_ref, square_ref
):
    lane = lanes()
    sub = sublanes()
    rim = (lane < 4) | (lane >= 124)
    blank = jnp.zeros((EXT_ROWS, EXT_COLS), F32)
    for ref in (k_ref, v0_ref, v1_ref, v2_ref):
        ref[LAYERS] = blank

    def spread(tile, place):
        return jnp.where(rim, pltpu.roll(tile, (252 - place) % 128, axis=1), 0.0)

    low_edges = low_ref[32]
    high_edges = high_ref[32]
    halo_edges = (
        jnp.where(sub < 4, high_edges, low_edges),
        pltpu.roll(jnp.where(sub < 4, low_edges, high_edges), 4, axis=0),
    )
    for l in range(LAYERS):
        edge = recv_ref[l, 8]
        for q, ref in enumerate((k_ref, v0_ref)):
            for g in range(2):
                for t in range(2):
                    ref[l, 8 * g : 8 * g + 8, 128 * t : 128 * t + 128] = recv_ref[l, 4 * q + 2 * g + t]
                ref[l, 8 * g : 8 * g + 8, 256:384] = spread(edge, 8 * (2 * g + q))
            ref[l, 16:24, 256:384] = spread(halo_edges[l // 8], 16 * (l % 8) + 8 * q)
        for t in range(2):
            cols = slice(128 * t, 128 * t + 128)
            high = high_ref[2 * l + t]
            low = low_ref[2 * l + t]
            k_ref[l, 16:24, cols] = jnp.where(sub < 4, high, low)
            v0_ref[l, 16:24, cols] = pltpu.roll(jnp.where(sub < 4, low, high), 4, axis=0)

    def setup(l, carry):
        cz_before, s0, m0 = carry
        k = k_ref[l]
        cc = k + pltpu.roll(k, EXT_COLS - 1, axis=1)
        cr = k + pltpu.roll(k, EXT_ROWS - 1, axis=0)
        cz = k + k_ref[l + 1]
        diag = (cc + pltpu.roll(cc, 1, axis=1)) + (cr + pltpu.roll(cr, 1, axis=0)) + (cz + cz_before)
        inv = jnp.where(k > 0.0, 1.0 / diag, 0.0)
        twice = v0_ref[l] * 2.0
        v0 = twice * inv
        cc_ref[l] = cc
        cr_ref[l] = cr
        cz_ref[l] = cz
        inv_ref[l] = inv
        v0_ref[l] = v0
        mine = own(v0)
        for g in range(2):
            for t in range(2):
                ret_ref[l, 2 * g + t] = mine[8 * g : 8 * g + 8, 128 * t : 128 * t + 128]
        return cz, s0 + folded(mine * own(twice)), m0 + mine

    none = jnp.zeros((8, 128), F32)
    no_map = jnp.zeros((ROWS, WIDTH), F32)
    _, s0, m0 = lax.fori_loop(0, LAYERS, setup, (k_ref[0], none, no_map), unroll=4)

    def image(l, v_ref, fz_before):
        v = v_ref[l]
        fc = cc_ref[l] * (v - pltpu.roll(v, EXT_COLS - 1, axis=1))
        fr = cr_ref[l] * (v - pltpu.roll(v, EXT_ROWS - 1, axis=0))
        fz = cz_ref[l] * (v - v_ref[l + 1])
        result = (fc - pltpu.roll(fc, 1, axis=1)) + (fr - pltpu.roll(fr, 1, axis=0)) + (fz - fz_before)
        return v, result, fz

    def step(v_ref, out_ref, slot):
        def body(l, carry):
            fz_before, odd, even, total = carry
            v, result, fz = image(l, v_ref, fz_before)
            after = inv_ref[l] * result
            out_ref[l] = after
            mine = own(after)
            for g in range(2):
                for t in range(2):
                    ret_ref[l, 4 * slot + 2 * g + t] = mine[8 * g : 8 * g + 8, 128 * t : 128 * t + 128]
            got = own(result)
            return fz, odd + folded(own(v) * got), even + folded(mine * got), total + mine

        start = (-(k_ref[0] * v_ref[0]), none, none, no_map)
        return lax.fori_loop(0, LAYERS, body, start, unroll=4)[1:]

    s1, s2, m1 = step(v0_ref, v1_ref, 1)
    s3, s4, m2 = step(v1_ref, v2_ref, 2)

    def last(l, carry):
        fz_before, odd = carry
        v, result, fz = image(l, v2_ref, fz_before)
        return fz, odd + folded(own(v) * own(result))

    _, s5 = lax.fori_loop(0, LAYERS, last, (-(k_ref[0] * v2_ref[0]), none), unroll=4)

    sums = none
    for n, part in enumerate((s0, s1, s2, s3, s4, s5)):
        sums = jnp.where(sub == n, jnp.sum(part), sums)
    for t in range(2):
        for f, total in enumerate((m0, m1, m2)):
            square_ref[48 * t + 16 * f : 48 * t + 16 * f + 16, :] = total[:, 128 * t : 128 * t + 128]
    square_ref[96:104, :] = sums
    square_ref[104:128, :] = jnp.zeros((24, 128), F32)
    turned = square_ref[...].T
    for j in range(LAYERS):
        ret_ref[j, 12] = turned[8 * j : 8 * j + 8, :]


def tree(values):
    while len(values) > 1:
        values = [a + b for a, b in zip(values[::2], values[1::2])]
    return values[0]


def route_kernel(owner_ref, index_ref, recv_ref, msg_ref):
    lane = lanes()
    total = tree([recv_ref[j, 12] for j in range(LAYERS)])
    common = pltpu.roll(total, 80, axis=1)
    for o in range(SLABS):
        msg_ref[o] = common[:4]
    row = index_ref[0] // PER_TILE
    for c in range(TILE_COLS):
        strip = recv_ref[c // 2, 12]
        first = pltpu.roll(strip, 80, axis=1) if c % 2 else strip
        second = pltpu.roll(pltpu.roll(strip, 16 if c % 2 else 64, axis=1), 4, axis=0)
        both = jnp.where(lane < 48, first, jnp.where(lane < 64, common, second))
        msg_ref[owner_ref[row, c]] = both[:4]


def weights(s):
    s0, s1, s2, s3, s4, s5 = s
    a0 = s0 / s1
    z1 = -a0
    n1 = s0 + z1 * (2.0 * s1 + z1 * s2)
    b0 = n1 / s0
    p0, p1 = 1.0 + b0, z1
    a1 = n1 / (p0 * p0 * s1 + p1 * (2.0 * p0 * s2 + p1 * s3))
    x0, x1 = a0 + a1 * p0, a1 * p1
    z1, z2 = z1 - a1 * p0, -(a1 * p1)
    n2 = s0 + z1 * (2.0 * s1 + z1 * s2) + z2 * (2.0 * (s2 + z1 * s3) + z2 * s4)
    b1 = n2 / n1
    p0, p1, p2 = 1.0 + b1 * p0, z1 + b1 * p1, z2
    energy = p0 * p0 * s1 + p1 * (2.0 * p0 * s2 + p1 * s3) + p2 * (2.0 * (p0 * s3 + p1 * s4) + p2 * s5)
    a2 = n2 / energy
    return x0 + a2 * p0, x1 + a2 * p1, a2 * p2


def finish_kernel(rows_ref, recv_ref, ret_ref, adjoint_ref, owned_ref):
    lane = lanes()
    sub = sublanes()
    total = tree([recv_ref[s] for s in range(SLABS)])
    moments = [jnp.broadcast_to(total[:1, 48 + n : 49 + n], (8, 128)) for n in range(6)]
    w0, w1, w2 = weights(moments)
    for j in range(LAYERS):
        for g in range(2):
            for t in range(2):
                n = 2 * g + t
                value = w0 * ret_ref[j, n] + w1 * ret_ref[j, 4 + n] + w2 * ret_ref[j, 8 + n]
                col = WIDTH * j + 128 * t
                adjoint_ref[0, 8 * g : 8 * g + 8, col : col + 128] = value
    for k in range(OWNED):
        row = rows_ref[k]
        tile = jnp.zeros((8, 128), F32)
        for i in range(PER_TILE):
            half = recv_ref[PER_TILE * row + i]
            whole = jnp.concatenate([half, half], axis=0)
            strip = jnp.where(sub < 4, whole, pltpu.roll(whole, 64, axis=1))
            value = w0 * strip + w1 * pltpu.roll(strip, 112, axis=1) + w2 * pltpu.roll(strip, 96, axis=1)
            if i:
                value = pltpu.roll(value, 16 * i, axis=1)
            tile = jnp.where((lane >= 16 * i) & (lane < 16 * i + 16), value, tile)
        owned_ref[k] = tile


VMEM = pl.BlockSpec(memory_space=pltpu.VMEM)
SMEM = pl.BlockSpec(memory_space=pltpu.SMEM)


def shape(*dims):
    return jax.ShapeDtypeStruct(dims, F32)


def call(kernel, ins, outs, scratch=(), interpret=False):
    single = len(outs) == 1
    return pl.pallas_call(
        kernel,
        out_shape=outs[0] if single else tuple(outs),
        in_specs=ins,
        out_specs=VMEM if single else tuple(VMEM for _ in outs),
        scratch_shapes=list(scratch),
        compiler_params=pltpu.CompilerParams(vmem_limit_bytes=VMEM_LIMIT),
        interpret=interpret,
    )


def pack(cond, src, interpret=False):
    return call(pack_kernel, [VMEM] * 2, [shape(LAYERS, 9, 8, 128)], interpret=interpret)(cond, src)


def halo(recv, interpret=False):
    side = shape(2 * LAYERS + 1, 8, 128)
    return call(halo_kernel, [VMEM], [side, side], interpret=interpret)(recv)


def krylov(recv, low, high, interpret=False):
    field = pltpu.VMEM((LAYERS + 1, EXT_ROWS, EXT_COLS), F32)
    face = pltpu.VMEM((LAYERS, EXT_ROWS, EXT_COLS), F32)
    return call(
        krylov_kernel,
        [VMEM] * 3,
        [shape(LAYERS, 13, 8, 128)],
        [field] * 4 + [face] * 4 + [pltpu.VMEM((128, 128), F32)],
        interpret=interpret,
    )(recv, low, high)


def route(owner, index, recv, interpret=False):
    return call(route_kernel, [SMEM, SMEM, VMEM], [shape(SLABS, 4, 128)], interpret=interpret)(owner, index, recv)


def finish(rows, recv, ret, interpret=False):
    return call(
        finish_kernel, [SMEM, VMEM, VMEM], [shape(1, ROWS, COLS), shape(OWNED, 8, 128)], interpret=interpret
    )(rows, recv, ret)


def owned_rows(tile_owner, index):
    held = jnp.any(tile_owner == index, axis=1)
    rank = jnp.cumsum(held.astype(jnp.int32)) - 1
    slot = jnp.arange(OWNED, dtype=jnp.int32)[:, None]
    row = jnp.arange(tile_owner.shape[0], dtype=jnp.int32)[None, :]
    return jnp.sum(jnp.where(held[None, :] & (rank[None, :] == slot), row, 0), axis=1)


def per_device(adjoint_source, conductivity, tile_owner):
    index = lax.axis_index("slab")
    count = lax.axis_size("slab")
    recv = lax.all_to_all(pack(conductivity, adjoint_source), "layer", 0, 0, tiled=True)
    up, down = halo(recv)
    low = lax.ppermute(up, "slab", [(i, i + 1) for i in range(count - 1)])
    high = lax.ppermute(down, "slab", [(i + 1, i) for i in range(count - 1)])
    back = lax.all_to_all(krylov(recv, low, high), "layer", 0, 0, tiled=True)
    outgoing = route(tile_owner, index.reshape(1), back)
    received = lax.all_to_all(outgoing, "slab", 0, 0, tiled=True)
    return finish(owned_rows(tile_owner, index), received, back)


def solution(mesh):
    placed = (P("layer", "slab", None), P("layer", "slab", None), P())
    return jax.shard_map(
        per_device,
        mesh=mesh,
        in_specs=placed,
        out_specs=(P("layer", "slab", None), P("slab", "layer", None)),
        check_vma=False,
    )
```

```python
import jax
import jax.numpy as jnp
from jax import lax
from jax.experimental import pallas as pl
from jax.experimental.pallas import tpu as pltpu
from jax.sharding import PartitionSpec as P

F32 = jnp.float32
LAYERS = 16
ROWS = 16
COLS = 4096
WIDTH = COLS // LAYERS
SLABS = 64
TILE_COLS = 32
PER_TILE = 8
OWNED = 4
EXT_ROWS = 24
EXT_COLS = 384
VMEM_LIMIT = 48 * 1024 * 1024


def lanes():
    return lax.broadcasted_iota(jnp.int32, (8, 128), 1)


def sublanes():
    return lax.broadcasted_iota(jnp.int32, (8, 128), 0)


def pack_kernel(cond_ref, src_ref, out_ref):
    lane = lanes()
    zero = jnp.zeros((8, 128), F32)
    for j in range(LAYERS):
        edge = zero
        for q, ref in enumerate((cond_ref, src_ref)):
            for g in range(2):
                rows = slice(8 * g, 8 * g + 8)
                base = WIDTH * j
                for t in range(2):
                    out_ref[j, 4 * q + 2 * g + t] = ref[0, rows, base + 128 * t : base + 128 * t + 128]
                before = ref[0, rows, base - 128 : base] if j > 0 else zero
                after = ref[0, rows, base + 256 : base + 384] if j < LAYERS - 1 else zero
                both = jnp.where(lane < 4, after, jnp.where(lane >= 124, before, 0.0))
                edge = edge + pltpu.roll(both, 4 + 8 * (2 * g + q), axis=1)
        out_ref[j, 8] = edge


def halo_kernel(recv_ref, up_ref, down_ref):
    lane = lanes()
    sub = sublanes()
    up_edges = [jnp.zeros((8, 128), F32)] * 2
    down_edges = [jnp.zeros((8, 128), F32)] * 2
    for l in range(LAYERS):
        for t in range(2):
            up_ref[2 * l + t] = jnp.where(sub >= 4, recv_ref[l, 2 + t], pltpu.roll(recv_ref[l, 6 + t], 4, axis=0))
            down_ref[2 * l + t] = jnp.where(sub < 4, recv_ref[l, t], pltpu.roll(recv_ref[l, 4 + t], 4, axis=0))
        edge = recv_ref[l, 8]
        half, place = l // 8, 16 * (l % 8)
        here = (lane >= place) & (lane < place + 16)
        up_edges[half] = jnp.where(here, pltpu.roll(edge, (place + 112) % 128, axis=1), up_edges[half])
        down_edges[half] = jnp.where(here, pltpu.roll(edge, place, axis=1), down_edges[half])
    up_ref[32] = jnp.where(sub >= 4, up_edges[0], pltpu.roll(up_edges[1], 4, axis=0))
    down_ref[32] = jnp.where(sub < 4, down_edges[0], pltpu.roll(down_edges[1], 4, axis=0))


def own(value):
    return value[:ROWS, :WIDTH]


def folded(value):
    return (value[:8, :128] + value[8:, :128]) + (value[:8, 128:] + value[8:, 128:])


def krylov_kernel(
    index_ref, recv_ref, low_ref, high_ref, ret_ref, k_ref, v0_ref, v1_ref, v2_ref, inv_ref, cc_ref, cr_ref, cz_ref, square_ref
):
    lane = lanes()
    sub = sublanes()
    rim = (lane < 4) | (lane >= 124)
    blank = jnp.zeros((EXT_ROWS, EXT_COLS), F32)
    for ref in (k_ref, v0_ref, v1_ref, v2_ref):
        ref[LAYERS] = blank

    def spread(tile, place):
        return jnp.where(rim, pltpu.roll(tile, (252 - place) % 128, axis=1), 0.0)

    inside = ((sub < 4) & (index_ref[0] < SLABS - 1)) | ((sub >= 4) & (index_ref[0] > 0))
    low_edges = low_ref[32]
    high_edges = high_ref[32]
    halo_edges = (
        jnp.where(sub < 4, high_edges, low_edges),
        pltpu.roll(jnp.where(sub < 4, low_edges, high_edges), 4, axis=0),
    )
    for l in range(LAYERS):
        edge = recv_ref[l, 8]
        for q, ref in enumerate((k_ref, v0_ref)):
            for g in range(2):
                for t in range(2):
                    ref[l, 8 * g : 8 * g + 8, 128 * t : 128 * t + 128] = recv_ref[l, 4 * q + 2 * g + t]
                ref[l, 8 * g : 8 * g + 8, 256:384] = spread(edge, 8 * (2 * g + q))
            ref[l, 16:24, 256:384] = jnp.where(inside, spread(halo_edges[l // 8], 16 * (l % 8) + 8 * q), 0.0)
        for t in range(2):
            cols = slice(128 * t, 128 * t + 128)
            high = high_ref[2 * l + t]
            low = low_ref[2 * l + t]
            k_ref[l, 16:24, cols] = jnp.where(inside, jnp.where(sub < 4, high, low), 0.0)
            v0_ref[l, 16:24, cols] = jnp.where(inside, pltpu.roll(jnp.where(sub < 4, low, high), 4, axis=0), 0.0)

    def setup(l, carry):
        cz_before, s0, m0 = carry
        k = k_ref[l]
        cc = k + pltpu.roll(k, EXT_COLS - 1, axis=1)
        cr = k + pltpu.roll(k, EXT_ROWS - 1, axis=0)
        cz = k + k_ref[l + 1]
        diag = (cc + pltpu.roll(cc, 1, axis=1)) + (cr + pltpu.roll(cr, 1, axis=0)) + (cz + cz_before)
        inv = jnp.where(k > 0.0, 1.0 / diag, 0.0)
        twice = v0_ref[l] * 2.0
        v0 = twice * inv
        cc_ref[l] = cc
        cr_ref[l] = cr
        cz_ref[l] = cz
        inv_ref[l] = inv
        v0_ref[l] = v0
        mine = own(v0)
        for g in range(2):
            for t in range(2):
                ret_ref[l, 2 * g + t] = mine[8 * g : 8 * g + 8, 128 * t : 128 * t + 128]
        return cz, s0 + folded(mine * own(twice)), m0 + mine

    none = jnp.zeros((8, 128), F32)
    no_map = jnp.zeros((ROWS, WIDTH), F32)
    _, s0, m0 = lax.fori_loop(0, LAYERS, setup, (k_ref[0], none, no_map), unroll=8)

    def image(l, v_ref, fz_before):
        v = v_ref[l]
        fc = cc_ref[l] * (v - pltpu.roll(v, EXT_COLS - 1, axis=1))
        fr = cr_ref[l] * (v - pltpu.roll(v, EXT_ROWS - 1, axis=0))
        fz = cz_ref[l] * (v - v_ref[l + 1])
        result = (fc - pltpu.roll(fc, 1, axis=1)) + (fr - pltpu.roll(fr, 1, axis=0)) + (fz - fz_before)
        return v, result, fz

    def step(v_ref, out_ref, slot):
        def body(l, carry):
            fz_before, odd, even, total = carry
            v, result, fz = image(l, v_ref, fz_before)
            after = inv_ref[l] * result
            out_ref[l] = after
            mine = own(after)
            for g in range(2):
                for t in range(2):
                    ret_ref[l, 4 * slot + 2 * g + t] = mine[8 * g : 8 * g + 8, 128 * t : 128 * t + 128]
            got = own(result)
            return fz, odd + folded(own(v) * got), even + folded(mine * got), total + mine

        start = (-(k_ref[0] * v_ref[0]), none, none, no_map)
        return lax.fori_loop(0, LAYERS, body, start, unroll=8)[1:]

    s1, s2, m1 = step(v0_ref, v1_ref, 1)
    s3, s4, m2 = step(v1_ref, v2_ref, 2)

    def last(l, carry):
        fz_before, odd = carry
        v, result, fz = image(l, v2_ref, fz_before)
        return fz, odd + folded(own(v) * own(result))

    _, s5 = lax.fori_loop(0, LAYERS, last, (-(k_ref[0] * v2_ref[0]), none), unroll=8)

    sums = none
    for n, part in enumerate((s0, s1, s2, s3, s4, s5)):
        sums = jnp.where(sub == n, jnp.sum(part), sums)
    first = lax.broadcasted_iota(jnp.int32, (ROWS, 128), 1) % 8 < 4
    for f, total in enumerate((m0, m1, m2)):
        left, right = total[:, :128], total[:, 128:]
        square_ref[16 * f : 16 * f + 16, :] = jnp.where(first, left, pltpu.roll(right, 4, axis=1))
        square_ref[64 + 16 * f : 80 + 16 * f, :] = jnp.where(first, pltpu.roll(left, 124, axis=1), right)
    square_ref[48:56, :] = sums
    square_ref[56:64, :] = none
    square_ref[112:120, :] = none
    square_ref[120:128, :] = none
    turned = square_ref[...].T
    for j in range(LAYERS):
        ret_ref[j, 12] = turned[8 * j : 8 * j + 8, :]


def tree(values):
    while len(values) > 1:
        values = [a + b for a, b in zip(values[::2], values[1::2])]
    return values[0]


def route_kernel(owner_ref, index_ref, recv_ref, msg_ref):
    lane = lax.broadcasted_iota(jnp.int32, (4, 128), 1)
    shared = (lane >= 48) & (lane < 64)
    total = tree([recv_ref[j, 12] for j in range(LAYERS)])
    common = total[:4]
    for o in range(SLABS):
        msg_ref[o] = common
    row = index_ref[0] // PER_TILE
    for c in range(TILE_COLS):
        half = 4 * (c % 2)
        strip = recv_ref[c // 2, 12, half : half + 4]
        msg_ref[owner_ref[row, c]] = jnp.where(shared, common, strip)


def weights(s):
    s0, s1, s2, s3, s4, s5 = s
    a0 = s0 / s1
    z1 = -a0
    n1 = s0 + z1 * (2.0 * s1 + z1 * s2)
    b0 = n1 / s0
    p0, p1 = 1.0 + b0, z1
    a1 = n1 / (p0 * p0 * s1 + p1 * (2.0 * p0 * s2 + p1 * s3))
    x0, x1 = a0 + a1 * p0, a1 * p1
    z1, z2 = z1 - a1 * p0, -(a1 * p1)
    n2 = s0 + z1 * (2.0 * s1 + z1 * s2) + z2 * (2.0 * (s2 + z1 * s3) + z2 * s4)
    b1 = n2 / n1
    p0, p1, p2 = 1.0 + b1 * p0, z1 + b1 * p1, z2
    energy = p0 * p0 * s1 + p1 * (2.0 * p0 * s2 + p1 * s3) + p2 * (2.0 * (p0 * s3 + p1 * s4) + p2 * s5)
    a2 = n2 / energy
    return x0 + a2 * p0, x1 + a2 * p1, a2 * p2


def finish_kernel(rows_ref, recv_ref, ret_ref, adjoint_ref, owned_ref):
    lane = lanes()
    sub = sublanes()
    total = tree([recv_ref[s] for s in range(SLABS)])
    moments = [jnp.broadcast_to(total[:1, 48 + n : 49 + n], (8, 128)) for n in range(6)]
    w0, w1, w2 = weights(moments)
    for j in range(LAYERS):
        for g in range(2):
            for t in range(2):
                n = 2 * g + t
                value = w0 * ret_ref[j, n] + w1 * ret_ref[j, 4 + n] + w2 * ret_ref[j, 8 + n]
                col = WIDTH * j + 128 * t
                adjoint_ref[0, 8 * g : 8 * g + 8, col : col + 128] = value
    for k in range(OWNED):
        row = rows_ref[k]
        tile = jnp.zeros((8, 128), F32)
        for i in range(PER_TILE):
            half = recv_ref[PER_TILE * row + i]
            whole = jnp.concatenate([half, half], axis=0)
            strip = jnp.where(sub < 4, whole, pltpu.roll(whole, 64, axis=1))
            value = w0 * strip + w1 * pltpu.roll(strip, 112, axis=1) + w2 * pltpu.roll(strip, 96, axis=1)
            if i:
                value = pltpu.roll(value, 16 * i, axis=1)
            tile = jnp.where((lane >= 16 * i) & (lane < 16 * i + 16), value, tile)
        owned_ref[k] = tile


VMEM = pl.BlockSpec(memory_space=pltpu.VMEM)
SMEM = pl.BlockSpec(memory_space=pltpu.SMEM)


def shape(*dims):
    return jax.ShapeDtypeStruct(dims, F32)


def call(kernel, ins, outs, scratch=(), interpret=False):
    single = len(outs) == 1
    return pl.pallas_call(
        kernel,
        out_shape=outs[0] if single else tuple(outs),
        in_specs=ins,
        out_specs=VMEM if single else tuple(VMEM for _ in outs),
        scratch_shapes=list(scratch),
        compiler_params=pltpu.CompilerParams(vmem_limit_bytes=VMEM_LIMIT),
        interpret=interpret,
    )


def pack(cond, src, interpret=False):
    return call(pack_kernel, [VMEM] * 2, [shape(LAYERS, 9, 8, 128)], interpret=interpret)(cond, src)


def halo(recv, interpret=False):
    side = shape(2 * LAYERS + 1, 8, 128)
    return call(halo_kernel, [VMEM], [side, side], interpret=interpret)(recv)


def krylov(index, recv, low, high, interpret=False):
    field = pltpu.VMEM((LAYERS + 1, EXT_ROWS, EXT_COLS), F32)
    face = pltpu.VMEM((LAYERS, EXT_ROWS, EXT_COLS), F32)
    return call(
        krylov_kernel,
        [SMEM] + [VMEM] * 3,
        [shape(LAYERS, 13, 8, 128)],
        [field] * 4 + [face] * 4 + [pltpu.VMEM((128, 128), F32)],
        interpret=interpret,
    )(index, recv, low, high)


def route(owner, index, recv, interpret=False):
    return call(route_kernel, [SMEM, SMEM, VMEM], [shape(SLABS, 4, 128)], interpret=interpret)(owner, index, recv)


def finish(rows, recv, ret, interpret=False):
    return call(
        finish_kernel, [SMEM, VMEM, VMEM], [shape(1, ROWS, COLS), shape(OWNED, 8, 128)], interpret=interpret
    )(rows, recv, ret)


def owned_rows(tile_owner, index):
    held = jnp.any(tile_owner == index, axis=1)
    rank = jnp.cumsum(held.astype(jnp.int32)) - 1
    slot = jnp.arange(OWNED, dtype=jnp.int32)[:, None]
    row = jnp.arange(tile_owner.shape[0], dtype=jnp.int32)[None, :]
    return jnp.sum(jnp.where(held[None, :] & (rank[None, :] == slot), row, 0), axis=1)


def per_device(adjoint_source, conductivity, tile_owner):
    index = lax.axis_index("slab")
    count = lax.axis_size("slab")
    recv = lax.all_to_all(pack(conductivity, adjoint_source), "layer", 0, 0, tiled=True)
    up, down = halo(recv)
    place = index.reshape(1)
    low = lax.ppermute(up, "slab", [(i, (i + 1) % count) for i in range(count)])
    high = lax.ppermute(down, "slab", [((i + 1) % count, i) for i in range(count)])
    back = lax.all_to_all(krylov(place, recv, low, high), "layer", 0, 0, tiled=True)
    outgoing = route(tile_owner, place, back)
    received = lax.all_to_all(outgoing, "slab", 0, 0, tiled=True)
    return finish(owned_rows(tile_owner, index), received, back)


def solution(mesh):
    placed = (P("layer", "slab", None), P("layer", "slab", None), P())
    return jax.shard_map(
        per_device,
        mesh=mesh,
        in_specs=placed,
        out_specs=(P("layer", "slab", None), P("slab", "layer", None)),
        check_vma=False,
    )
```

```python
import jax
import jax.numpy as jnp
from jax import lax
from jax.experimental import pallas as pl
from jax.experimental.pallas import tpu as pltpu
from jax.sharding import PartitionSpec as P

F32 = jnp.float32
LAYERS = 16
ROWS = 16
COLS = 4096
WIDTH = COLS // LAYERS
SLABS = 64
TILE_COLS = 32
PER_TILE = 8
OWNED = 4
EXT_ROWS = 24
EXT_COLS = 384
VMEM_LIMIT = 48 * 1024 * 1024


def lanes():
    return lax.broadcasted_iota(jnp.int32, (8, 128), 1)


def sublanes():
    return lax.broadcasted_iota(jnp.int32, (8, 128), 0)


def pack_kernel(both_ref, out_ref):
    lane = lanes()
    zero = jnp.zeros((8, 128), F32)
    for j in range(LAYERS):
        edge = zero
        for q in range(2):
            for g in range(2):
                rows = slice(8 * g, 8 * g + 8)
                base = WIDTH * j
                for t in range(2):
                    out_ref[j, 4 * q + 2 * g + t] = both_ref[q, rows, base + 128 * t : base + 128 * t + 128]
                before = both_ref[q, rows, base - 128 : base] if j > 0 else zero
                after = both_ref[q, rows, base + 256 : base + 384] if j < LAYERS - 1 else zero
                both = jnp.where(lane < 4, after, jnp.where(lane >= 124, before, 0.0))
                edge = edge + pltpu.roll(both, 4 + 8 * (2 * g + q), axis=1)
        out_ref[j, 8] = edge


def halo_kernel(recv_ref, up_ref, down_ref):
    lane = lanes()
    sub = sublanes()
    up_edges = [jnp.zeros((8, 128), F32)] * 2
    down_edges = [jnp.zeros((8, 128), F32)] * 2
    for l in range(LAYERS):
        for t in range(2):
            up_ref[2 * l + t] = jnp.where(sub >= 4, recv_ref[l, 2 + t], pltpu.roll(recv_ref[l, 6 + t], 4, axis=0))
            down_ref[2 * l + t] = jnp.where(sub < 4, recv_ref[l, t], pltpu.roll(recv_ref[l, 4 + t], 4, axis=0))
        edge = recv_ref[l, 8]
        half, place = l // 8, 16 * (l % 8)
        here = (lane >= place) & (lane < place + 16)
        up_edges[half] = jnp.where(here, pltpu.roll(edge, (place + 112) % 128, axis=1), up_edges[half])
        down_edges[half] = jnp.where(here, pltpu.roll(edge, place, axis=1), down_edges[half])
    up_ref[32] = jnp.where(sub >= 4, up_edges[0], pltpu.roll(up_edges[1], 4, axis=0))
    down_ref[32] = jnp.where(sub < 4, down_edges[0], pltpu.roll(down_edges[1], 4, axis=0))


def own(value):
    return value[:ROWS, :WIDTH]


def folded(value):
    return (value[:8, :128] + value[8:, :128]) + (value[:8, 128:] + value[8:, 128:])


def krylov_kernel(
    index_ref, rows_ref, recv_ref, low_ref, high_ref, msg_ref, ret_ref, k_ref, v0_ref, v1_ref, v2_ref, inv_ref, cc_ref, cr_ref, cz_ref, square_ref
):
    lane = lanes()
    sub = sublanes()
    rim = (lane < 4) | (lane >= 124)
    blank = jnp.zeros((EXT_ROWS, EXT_COLS), F32)
    for ref in (k_ref, v0_ref, v1_ref, v2_ref):
        ref[LAYERS] = blank

    def spread(tile, place):
        return jnp.where(rim, pltpu.roll(tile, (252 - place) % 128, axis=1), 0.0)

    inside = ((sub < 4) & (index_ref[0] < SLABS - 1)) | ((sub >= 4) & (index_ref[0] > 0))
    low_edges = low_ref[32]
    high_edges = high_ref[32]
    halo_edges = (
        jnp.where(sub < 4, high_edges, low_edges),
        pltpu.roll(jnp.where(sub < 4, low_edges, high_edges), 4, axis=0),
    )
    for l in range(LAYERS):
        edge = recv_ref[l, 8]
        for q, ref in enumerate((k_ref, v0_ref)):
            for g in range(2):
                for t in range(2):
                    ref[l, 8 * g : 8 * g + 8, 128 * t : 128 * t + 128] = recv_ref[l, 4 * q + 2 * g + t]
                ref[l, 8 * g : 8 * g + 8, 256:384] = spread(edge, 8 * (2 * g + q))
            ref[l, 16:24, 256:384] = jnp.where(inside, spread(halo_edges[l // 8], 16 * (l % 8) + 8 * q), 0.0)
        for t in range(2):
            cols = slice(128 * t, 128 * t + 128)
            high = high_ref[2 * l + t]
            low = low_ref[2 * l + t]
            k_ref[l, 16:24, cols] = jnp.where(inside, jnp.where(sub < 4, high, low), 0.0)
            v0_ref[l, 16:24, cols] = jnp.where(inside, pltpu.roll(jnp.where(sub < 4, low, high), 4, axis=0), 0.0)

    def setup(l, carry):
        cz_before, s0, m0 = carry
        k = k_ref[l]
        cc = k + pltpu.roll(k, EXT_COLS - 1, axis=1)
        cr = k + pltpu.roll(k, EXT_ROWS - 1, axis=0)
        cz = k + k_ref[l + 1]
        diag = (cc + pltpu.roll(cc, 1, axis=1)) + (cr + pltpu.roll(cr, 1, axis=0)) + (cz + cz_before)
        inv = jnp.where(k > 0.0, 1.0 / diag, 0.0)
        twice = v0_ref[l] * 2.0
        v0 = twice * inv
        cc_ref[l] = cc
        cr_ref[l] = cr
        cz_ref[l] = cz
        inv_ref[l] = inv
        v0_ref[l] = v0
        mine = own(v0)
        for g in range(2):
            for t in range(2):
                ret_ref[l, 2 * g + t] = mine[8 * g : 8 * g + 8, 128 * t : 128 * t + 128]
        return cz, s0 + folded(mine * own(twice)), m0 + mine

    none = jnp.zeros((8, 128), F32)
    no_map = jnp.zeros((ROWS, WIDTH), F32)
    _, s0, m0 = lax.fori_loop(0, LAYERS, setup, (k_ref[0], none, no_map), unroll=8)

    def image(l, v_ref, fz_before):
        v = v_ref[l]
        fc = cc_ref[l] * (v - pltpu.roll(v, EXT_COLS - 1, axis=1))
        fr = cr_ref[l] * (v - pltpu.roll(v, EXT_ROWS - 1, axis=0))
        fz = cz_ref[l] * (v - v_ref[l + 1])
        result = (fc - pltpu.roll(fc, 1, axis=1)) + (fr - pltpu.roll(fr, 1, axis=0)) + (fz - fz_before)
        return v, result, fz

    def step(v_ref, out_ref, slot):
        def body(l, carry):
            fz_before, odd, even, total = carry
            v, result, fz = image(l, v_ref, fz_before)
            after = inv_ref[l] * result
            out_ref[l] = after
            mine = own(after)
            for g in range(2):
                for t in range(2):
                    ret_ref[l, 4 * slot + 2 * g + t] = mine[8 * g : 8 * g + 8, 128 * t : 128 * t + 128]
            got = own(result)
            return fz, odd + folded(own(v) * got), even + folded(mine * got), total + mine

        start = (-(k_ref[0] * v_ref[0]), none, none, no_map)
        return lax.fori_loop(0, LAYERS, body, start, unroll=8)[1:]

    s1, s2, m1 = step(v0_ref, v1_ref, 1)
    s3, s4, m2 = step(v1_ref, v2_ref, 2)

    def last(l, carry):
        fz_before, odd = carry
        v, result, fz = image(l, v2_ref, fz_before)
        return fz, odd + folded(own(v) * own(result))

    _, s5 = lax.fori_loop(0, LAYERS, last, (-(k_ref[0] * v2_ref[0]), none), unroll=8)

    sums = none
    for n, part in enumerate((s0, s1, s2, s3, s4, s5)):
        sums = jnp.where(sub == n, jnp.sum(part), sums)
    first = lax.broadcasted_iota(jnp.int32, (ROWS, 128), 1) % 8 < 4
    for f, total in enumerate((m0, m1, m2)):
        left, right = total[:, :128], total[:, 128:]
        square_ref[16 * f : 16 * f + 16, :] = jnp.where(first, left, pltpu.roll(right, 4, axis=1))
        square_ref[64 + 16 * f : 80 + 16 * f, :] = jnp.where(first, pltpu.roll(left, 124, axis=1), right)
    square_ref[48:56, :] = sums
    square_ref[56:64, :] = none
    square_ref[112:120, :] = none
    square_ref[120:128, :] = none
    turned = square_ref[...].T
    for j in range(LAYERS):
        msg_ref[j] = turned[8 * j : 8 * j + 8, :]


def tree(values):
    while len(values) > 1:
        values = [a + b for a, b in zip(values[::2], values[1::2])]
    return values[0]


def route_kernel(owner_ref, index_ref, recv_ref, msg_ref):
    lane = lax.broadcasted_iota(jnp.int32, (4, 128), 1)
    shared = (lane >= 48) & (lane < 64)
    total = tree([recv_ref[j] for j in range(LAYERS)])
    common = total[:4]
    for o in range(SLABS):
        msg_ref[o] = common
    row = index_ref[0] // PER_TILE
    for c in range(TILE_COLS):
        half = 4 * (c % 2)
        strip = recv_ref[c // 2, half : half + 4]
        msg_ref[owner_ref[row, c]] = jnp.where(shared, common, strip)


def weights(s):
    s0, s1, s2, s3, s4, s5 = s
    a0 = s0 / s1
    z1 = -a0
    n1 = s0 + z1 * (2.0 * s1 + z1 * s2)
    b0 = n1 / s0
    p0, p1 = 1.0 + b0, z1
    a1 = n1 / (p0 * p0 * s1 + p1 * (2.0 * p0 * s2 + p1 * s3))
    x0, x1 = a0 + a1 * p0, a1 * p1
    z1, z2 = z1 - a1 * p0, -(a1 * p1)
    n2 = s0 + z1 * (2.0 * s1 + z1 * s2) + z2 * (2.0 * (s2 + z1 * s3) + z2 * s4)
    b1 = n2 / n1
    p0, p1, p2 = 1.0 + b1 * p0, z1 + b1 * p1, z2
    energy = p0 * p0 * s1 + p1 * (2.0 * p0 * s2 + p1 * s3) + p2 * (2.0 * (p0 * s3 + p1 * s4) + p2 * s5)
    a2 = n2 / energy
    return x0 + a2 * p0, x1 + a2 * p1, a2 * p2


def solved(recv_ref):
    total = tree([recv_ref[s] for s in range(SLABS)])
    return weights([jnp.broadcast_to(total[:1, 48 + n : 49 + n], (8, 128)) for n in range(6)])


def combine_kernel(recv_ref, ret_ref, out_ref):
    w0, w1, w2 = solved(recv_ref)
    for l in range(LAYERS):
        for n in range(4):
            out_ref[l, n] = w0 * ret_ref[l, n] + w1 * ret_ref[l, 4 + n] + w2 * ret_ref[l, 8 + n]


def finish_kernel(rows_ref, recv_ref, back_ref, adjoint_ref, owned_ref, full_ref, sems):
    lane = lanes()
    sub = sublanes()
    copies = []
    for part in range(4):
        for j in range(4 * part, 4 * part + 4):
            for n in range(4):
                col = WIDTH * j + 128 * (n % 2)
                full_ref[0, 8 * (n // 2) : 8 * (n // 2) + 8, col : col + 128] = back_ref[j, n]
        cols = slice(COLS // 4 * part, COLS // 4 * (part + 1))
        copy = pltpu.make_async_copy(full_ref.at[:, :, cols], adjoint_ref.at[:, :, cols], sems.at[part])
        copy.start()
        copies.append(copy)
    w0, w1, w2 = solved(recv_ref)
    for k in range(OWNED):
        row = rows_ref[k]
        tile = jnp.zeros((8, 128), F32)
        for i in range(PER_TILE):
            half = recv_ref[PER_TILE * row + i]
            whole = jnp.concatenate([half, half], axis=0)
            strip = jnp.where(sub < 4, whole, pltpu.roll(whole, 64, axis=1))
            value = w0 * strip + w1 * pltpu.roll(strip, 112, axis=1) + w2 * pltpu.roll(strip, 96, axis=1)
            if i:
                value = pltpu.roll(value, 16 * i, axis=1)
            tile = jnp.where((lane >= 16 * i) & (lane < 16 * i + 16), value, tile)
        owned_ref[k] = tile
    for copy in copies:
        copy.wait()


VMEM = pl.BlockSpec(memory_space=pltpu.VMEM)
SMEM = pl.BlockSpec(memory_space=pltpu.SMEM)


def shape(*dims):
    return jax.ShapeDtypeStruct(dims, F32)


def call(kernel, ins, outs, scratch=(), interpret=False, out_specs=None):
    single = len(outs) == 1
    if out_specs is None:
        out_specs = VMEM if single else tuple(VMEM for _ in outs)
    return pl.pallas_call(
        kernel,
        out_shape=outs[0] if single else tuple(outs),
        in_specs=ins,
        out_specs=out_specs,
        scratch_shapes=list(scratch),
        compiler_params=pltpu.CompilerParams(vmem_limit_bytes=VMEM_LIMIT),
        interpret=interpret,
    )


def pack(both, interpret=False):
    return call(pack_kernel, [VMEM], [shape(LAYERS, 9, 8, 128)], interpret=interpret)(both)


def halo(recv, interpret=False):
    side = shape(2 * LAYERS + 1, 8, 128)
    return call(halo_kernel, [VMEM], [side, side], interpret=interpret)(recv)


def krylov(index, rows, recv, low, high, interpret=False):
    field = pltpu.VMEM((LAYERS + 1, EXT_ROWS, EXT_COLS), F32)
    face = pltpu.VMEM((LAYERS, EXT_ROWS, EXT_COLS), F32)
    return call(
        krylov_kernel,
        [SMEM] * 2 + [VMEM] * 3,
        [shape(LAYERS, 8, 128), shape(LAYERS, 12, 8, 128)],
        [field] * 4 + [face] * 4 + [pltpu.VMEM((128, 128), F32)],
        interpret=interpret,
    )(index, rows, recv, low, high)


def route(owner, index, recv, interpret=False):
    return call(route_kernel, [SMEM, SMEM, VMEM], [shape(SLABS, 4, 128)], interpret=interpret)(owner, index, recv)


def combine(recv, ret, interpret=False):
    return call(combine_kernel, [VMEM] * 2, [shape(LAYERS, 4, 8, 128)], interpret=interpret)(recv, ret)


def finish(rows, recv, back, interpret=False):
    return call(
        finish_kernel,
        [SMEM, VMEM, VMEM],
        [shape(1, ROWS, COLS), shape(OWNED, 8, 128)],
        [pltpu.VMEM((1, ROWS, COLS), F32), pltpu.SemaphoreType.DMA((4,))],
        interpret=interpret,
        out_specs=(pl.BlockSpec(memory_space=pl.ANY), VMEM),
    )(rows, recv, back)


def owned_rows(tile_owner, index):
    held = jnp.any(tile_owner == index, axis=1)
    rank = jnp.cumsum(held.astype(jnp.int32)) - 1
    slot = jnp.arange(OWNED, dtype=jnp.int32)[:, None]
    row = jnp.arange(tile_owner.shape[0], dtype=jnp.int32)[None, :]
    return jnp.sum(jnp.where(held[None, :] & (rank[None, :] == slot), row, 0), axis=1)


def per_device(adjoint_source, conductivity, tile_owner):
    index = lax.axis_index("slab")
    count = lax.axis_size("slab")
    recv = lax.all_to_all(pack(jnp.concatenate([conductivity, adjoint_source], axis=0)), "layer", 0, 0, tiled=True)
    up, down = halo(recv)
    tile_owner, up = lax.optimization_barrier((tile_owner, up))
    rows = owned_rows(tile_owner, index)
    place = index.reshape(1)
    low = lax.ppermute(up, "slab", [(i, (i + 1) % count) for i in range(count)])
    high = lax.ppermute(down, "slab", [((i + 1) % count, i) for i in range(count)])
    msg, ret = krylov(place, rows, recv, low, high)
    strips = lax.all_to_all(msg, "layer", 0, 0, tiled=True)
    outgoing = route(tile_owner, place, strips)
    received = lax.all_to_all(outgoing, "slab", 0, 0, tiled=True)
    back = lax.all_to_all(combine(received, ret), "layer", 0, 0, tiled=True)
    return finish(rows, received, back)


def solution(mesh):
    placed = (P("layer", "slab", None), P("layer", "slab", None), P())
    return jax.shard_map(
        per_device,
        mesh=mesh,
        in_specs=placed,
        out_specs=(P("layer", "slab", None), P("slab", "layer", None)),
        check_vma=False,
    )
```

```python
import jax
import jax.numpy as jnp
from jax import lax
from jax.experimental import pallas as pl
from jax.experimental.pallas import tpu as pltpu
from jax.sharding import PartitionSpec as P

F32 = jnp.float32
LAYERS = 16
ROWS = 16
COLS = 4096
WIDTH = COLS // LAYERS
SLABS = 64
TILE_COLS = 32
PER_TILE = 8
OWNED = 4
EXT_ROWS = 24
EXT_COLS = 384
VMEM_LIMIT = 48 * 1024 * 1024


def lanes():
    return lax.broadcasted_iota(jnp.int32, (8, 128), 1)


def sublanes():
    return lax.broadcasted_iota(jnp.int32, (8, 128), 0)


def pack_kernel(both_ref, out_ref):
    lane = lanes()
    zero = jnp.zeros((8, 128), F32)
    for j in range(LAYERS):
        edge = zero
        for q in range(2):
            for g in range(2):
                rows = slice(8 * g, 8 * g + 8)
                base = WIDTH * j
                for t in range(2):
                    out_ref[j, 4 * q + 2 * g + t] = both_ref[q, rows, base + 128 * t : base + 128 * t + 128]
                before = both_ref[q, rows, base - 128 : base] if j > 0 else zero
                after = both_ref[q, rows, base + 256 : base + 384] if j < LAYERS - 1 else zero
                both = jnp.where(lane < 4, after, jnp.where(lane >= 124, before, 0.0))
                edge = edge + pltpu.roll(both, 4 + 8 * (2 * g + q), axis=1)
        out_ref[j, 8] = edge


def halo_kernel(index_ref, recv_ref, first_ref, second_ref):
    even = index_ref[0] % 2 == 0

    def put(n, up, down):
        first_ref[n] = jnp.where(even, up, down)
        second_ref[n] = jnp.where(even, down, up)

    lane = lanes()
    sub = sublanes()
    up_edges = [jnp.zeros((8, 128), F32)] * 2
    down_edges = [jnp.zeros((8, 128), F32)] * 2
    for l in range(LAYERS):
        for t in range(2):
            up = jnp.where(sub >= 4, recv_ref[l, 2 + t], pltpu.roll(recv_ref[l, 6 + t], 4, axis=0))
            down = jnp.where(sub < 4, recv_ref[l, t], pltpu.roll(recv_ref[l, 4 + t], 4, axis=0))
            put(2 * l + t, up, down)
        edge = recv_ref[l, 8]
        half, place = l // 8, 16 * (l % 8)
        here = (lane >= place) & (lane < place + 16)
        up_edges[half] = jnp.where(here, pltpu.roll(edge, (place + 112) % 128, axis=1), up_edges[half])
        down_edges[half] = jnp.where(here, pltpu.roll(edge, place, axis=1), down_edges[half])
    up = jnp.where(sub >= 4, up_edges[0], pltpu.roll(up_edges[1], 4, axis=0))
    down = jnp.where(sub < 4, down_edges[0], pltpu.roll(down_edges[1], 4, axis=0))
    put(32, up, down)


def own(value):
    return value[:ROWS, :WIDTH]


def folded(value):
    return (value[:8, :128] + value[8:, :128]) + (value[:8, 128:] + value[8:, 128:])


def krylov_kernel(
    index_ref, recv_ref, first_ref, second_ref, msg_ref, ret_ref, k_ref, v0_ref, v1_ref, v2_ref, inv_ref, cc_ref, cr_ref, cz_ref, square_ref
):
    lane = lanes()
    sub = sublanes()
    rim = (lane < 4) | (lane >= 124)
    blank = jnp.zeros((EXT_ROWS, EXT_COLS), F32)
    for ref in (k_ref, v0_ref, v1_ref, v2_ref):
        ref[LAYERS] = blank

    def spread(tile, place):
        return jnp.where(rim, pltpu.roll(tile, (252 - place) % 128, axis=1), 0.0)

    even = index_ref[0] % 2 == 0
    upper = (sub < 4) == even

    def halves(n):
        one, two = first_ref[n], second_ref[n]
        return jnp.where(upper, one, two), pltpu.roll(jnp.where(upper, two, one), 4, axis=0)

    halo_edges = halves(32)
    for l in range(LAYERS):
        edge = recv_ref[l, 8]
        for q, ref in enumerate((k_ref, v0_ref)):
            for g in range(2):
                for t in range(2):
                    ref[l, 8 * g : 8 * g + 8, 128 * t : 128 * t + 128] = recv_ref[l, 4 * q + 2 * g + t]
                ref[l, 8 * g : 8 * g + 8, 256:384] = spread(edge, 8 * (2 * g + q))
            ref[l, 16:24, 256:384] = spread(halo_edges[l // 8], 16 * (l % 8) + 8 * q)
        for t in range(2):
            cols = slice(128 * t, 128 * t + 128)
            k_ref[l, 16:24, cols], v0_ref[l, 16:24, cols] = halves(2 * l + t)

    def setup(l, carry):
        cz_before, s0, m0 = carry
        k = k_ref[l]
        cc = k + pltpu.roll(k, EXT_COLS - 1, axis=1)
        cr = k + pltpu.roll(k, EXT_ROWS - 1, axis=0)
        cz = k + k_ref[l + 1]
        diag = (cc + pltpu.roll(cc, 1, axis=1)) + (cr + pltpu.roll(cr, 1, axis=0)) + (cz + cz_before)
        inv = jnp.where(k > 0.0, 1.0 / diag, 0.0)
        twice = v0_ref[l] * 2.0
        v0 = twice * inv
        cc_ref[l] = cc
        cr_ref[l] = cr
        cz_ref[l] = cz
        inv_ref[l] = inv
        v0_ref[l] = v0
        mine = own(v0)
        for g in range(2):
            for t in range(2):
                ret_ref[l, 2 * g + t] = mine[8 * g : 8 * g + 8, 128 * t : 128 * t + 128]
        return cz, s0 + folded(mine * own(twice)), m0 + mine

    none = jnp.zeros((8, 128), F32)
    no_map = jnp.zeros((ROWS, WIDTH), F32)
    _, s0, m0 = lax.fori_loop(0, LAYERS, setup, (k_ref[0], none, no_map), unroll=8)

    def image(l, v_ref, fz_before):
        v = v_ref[l]
        fc = cc_ref[l] * (v - pltpu.roll(v, EXT_COLS - 1, axis=1))
        fr = cr_ref[l] * (v - pltpu.roll(v, EXT_ROWS - 1, axis=0))
        fz = cz_ref[l] * (v - v_ref[l + 1])
        result = (fc - pltpu.roll(fc, 1, axis=1)) + (fr - pltpu.roll(fr, 1, axis=0)) + (fz - fz_before)
        return v, result, fz

    def step(v_ref, out_ref, slot):
        def body(l, carry):
            fz_before, odd, even, total = carry
            v, result, fz = image(l, v_ref, fz_before)
            after = inv_ref[l] * result
            out_ref[l] = after
            mine = own(after)
            for g in range(2):
                for t in range(2):
                    ret_ref[l, 4 * slot + 2 * g + t] = mine[8 * g : 8 * g + 8, 128 * t : 128 * t + 128]
            got = own(result)
            return fz, odd + folded(own(v) * got), even + folded(mine * got), total + mine

        start = (-(k_ref[0] * v_ref[0]), none, none, no_map)
        return lax.fori_loop(0, LAYERS, body, start, unroll=8)[1:]

    s1, s2, m1 = step(v0_ref, v1_ref, 1)
    s3, s4, m2 = step(v1_ref, v2_ref, 2)

    def last(l, carry):
        fz_before, odd = carry
        v, result, fz = image(l, v2_ref, fz_before)
        return fz, odd + folded(own(v) * own(result))

    _, s5 = lax.fori_loop(0, LAYERS, last, (-(k_ref[0] * v2_ref[0]), none), unroll=8)

    sums = none
    for n, part in enumerate((s0, s1, s2, s3, s4, s5)):
        sums = jnp.where(sub == n, jnp.sum(part), sums)
    first = lax.broadcasted_iota(jnp.int32, (ROWS, 128), 1) % 8 < 4
    for f, total in enumerate((m0, m1, m2)):
        left, right = total[:, :128], total[:, 128:]
        square_ref[16 * f : 16 * f + 16, :] = jnp.where(first, left, pltpu.roll(right, 4, axis=1))
        square_ref[64 + 16 * f : 80 + 16 * f, :] = jnp.where(first, pltpu.roll(left, 124, axis=1), right)
    square_ref[48:56, :] = sums
    square_ref[56:64, :] = none
    square_ref[112:120, :] = none
    square_ref[120:128, :] = none
    turned = square_ref[...].T
    for j in range(LAYERS):
        msg_ref[j] = turned[8 * j : 8 * j + 8, :]


def tree(values):
    while len(values) > 1:
        values = [a + b for a, b in zip(values[::2], values[1::2])]
    return values[0]


def route_kernel(owner_ref, index_ref, recv_ref, msg_ref):
    lane = lax.broadcasted_iota(jnp.int32, (4, 128), 1)
    shared = (lane >= 48) & (lane < 64)
    total = tree([recv_ref[j] for j in range(LAYERS)])
    common = total[:4]
    for o in range(SLABS):
        msg_ref[o] = common
    row = index_ref[0] // PER_TILE
    for c in range(TILE_COLS):
        half = 4 * (c % 2)
        strip = recv_ref[c // 2, half : half + 4]
        msg_ref[owner_ref[row, c]] = jnp.where(shared, common, strip)


def weights(s):
    s0, s1, s2, s3, s4, s5 = s
    a0 = s0 / s1
    z1 = -a0
    n1 = s0 + z1 * (2.0 * s1 + z1 * s2)
    b0 = n1 / s0
    p0, p1 = 1.0 + b0, z1
    a1 = n1 / (p0 * p0 * s1 + p1 * (2.0 * p0 * s2 + p1 * s3))
    x0, x1 = a0 + a1 * p0, a1 * p1
    z1, z2 = z1 - a1 * p0, -(a1 * p1)
    n2 = s0 + z1 * (2.0 * s1 + z1 * s2) + z2 * (2.0 * (s2 + z1 * s3) + z2 * s4)
    b1 = n2 / n1
    p0, p1, p2 = 1.0 + b1 * p0, z1 + b1 * p1, z2
    energy = p0 * p0 * s1 + p1 * (2.0 * p0 * s2 + p1 * s3) + p2 * (2.0 * (p0 * s3 + p1 * s4) + p2 * s5)
    a2 = n2 / energy
    return x0 + a2 * p0, x1 + a2 * p1, a2 * p2


def solved(recv_ref):
    total = tree([recv_ref[s] for s in range(SLABS)])
    return weights([jnp.broadcast_to(total[:1, 48 + n : 49 + n], (8, 128)) for n in range(6)])


def combine_kernel(recv_ref, ret_ref, out_ref):
    w0, w1, w2 = solved(recv_ref)
    for l in range(LAYERS):
        for n in range(4):
            out_ref[l, n] = w0 * ret_ref[l, n] + w1 * ret_ref[l, 4 + n] + w2 * ret_ref[l, 8 + n]


def finish_kernel(rows_ref, recv_ref, back_ref, adjoint_ref, owned_ref):
    lane = lanes()
    sub = sublanes()
    for j in range(LAYERS):
        for n in range(4):
            col = WIDTH * j + 128 * (n % 2)
            adjoint_ref[0, 8 * (n // 2) : 8 * (n // 2) + 8, col : col + 128] = back_ref[j, n]
    w0, w1, w2 = solved(recv_ref)
    for k in range(OWNED):
        row = rows_ref[k]
        tile = jnp.zeros((8, 128), F32)
        for i in range(PER_TILE):
            half = recv_ref[PER_TILE * row + i]
            whole = jnp.concatenate([half, half], axis=0)
            strip = jnp.where(sub < 4, whole, pltpu.roll(whole, 64, axis=1))
            value = w0 * strip + w1 * pltpu.roll(strip, 112, axis=1) + w2 * pltpu.roll(strip, 96, axis=1)
            if i:
                value = pltpu.roll(value, 16 * i, axis=1)
            tile = jnp.where((lane >= 16 * i) & (lane < 16 * i + 16), value, tile)
        owned_ref[k] = tile


VMEM = pl.BlockSpec(memory_space=pltpu.VMEM)
SMEM = pl.BlockSpec(memory_space=pltpu.SMEM)


def shape(*dims):
    return jax.ShapeDtypeStruct(dims, F32)


def call(kernel, ins, outs, scratch=(), interpret=False):
    single = len(outs) == 1
    return pl.pallas_call(
        kernel,
        out_shape=outs[0] if single else tuple(outs),
        in_specs=ins,
        out_specs=VMEM if single else tuple(VMEM for _ in outs),
        scratch_shapes=list(scratch),
        compiler_params=pltpu.CompilerParams(vmem_limit_bytes=VMEM_LIMIT),
        interpret=interpret,
    )


def pack(both, interpret=False):
    return call(pack_kernel, [VMEM], [shape(LAYERS, 9, 8, 128)], interpret=interpret)(both)


def halo(index, recv, interpret=False):
    side = shape(2 * LAYERS + 1, 8, 128)
    return call(halo_kernel, [SMEM, VMEM], [side, side], interpret=interpret)(index, recv)


def krylov(index, recv, first, second, interpret=False):
    field = pltpu.VMEM((LAYERS + 1, EXT_ROWS, EXT_COLS), F32)
    face = pltpu.VMEM((LAYERS, EXT_ROWS, EXT_COLS), F32)
    return call(
        krylov_kernel,
        [SMEM] + [VMEM] * 3,
        [shape(LAYERS, 8, 128), shape(LAYERS, 12, 8, 128)],
        [field] * 4 + [face] * 4 + [pltpu.VMEM((128, 128), F32)],
        interpret=interpret,
    )(index, recv, first, second)


def route(owner, index, recv, interpret=False):
    return call(route_kernel, [SMEM, SMEM, VMEM], [shape(SLABS, 4, 128)], interpret=interpret)(owner, index, recv)


def combine(recv, ret, interpret=False):
    return call(combine_kernel, [VMEM] * 2, [shape(LAYERS, 4, 8, 128)], interpret=interpret)(recv, ret)


def finish(rows, recv, back, interpret=False):
    outs = [shape(1, ROWS, COLS), shape(OWNED, 8, 128)]
    return call(finish_kernel, [SMEM, VMEM, VMEM], outs, interpret=interpret)(rows, recv, back)


def owned_rows(tile_owner, index):
    held = jnp.any(tile_owner == index, axis=1)
    rank = jnp.cumsum(held.astype(jnp.int32)) - 1
    slot = jnp.arange(OWNED, dtype=jnp.int32)[:, None]
    row = jnp.arange(tile_owner.shape[0], dtype=jnp.int32)[None, :]
    return jnp.sum(jnp.where(held[None, :] & (rank[None, :] == slot), row, 0), axis=1)


def per_device(adjoint_source, conductivity, tile_owner):
    index = lax.axis_index("slab")
    place = index.reshape(1)
    count = lax.axis_size("slab")
    both = jnp.concatenate([conductivity, adjoint_source], axis=0)
    both, rows, tile_owner = lax.optimization_barrier((both, owned_rows(tile_owner, index), tile_owner))
    recv = lax.all_to_all(pack(both), "layer", 0, 0, tiled=True)
    first, second = halo(place, recv)
    meet = [(i, i + 1) for i in range(0, count - 1, 2)]
    part = [(i, i + 1) for i in range(1, count - 1, 2)]
    first = lax.ppermute(first, "slab", meet + [(j, i) for i, j in meet])
    second = lax.ppermute(second, "slab", part + [(j, i) for i, j in part])
    msg, ret = krylov(place, recv, first, second)
    strips = lax.all_to_all(msg, "layer", 0, 0, tiled=True)
    outgoing = route(tile_owner, place, strips)
    received = lax.all_to_all(outgoing, "slab", 0, 0, tiled=True)
    back = lax.all_to_all(combine(received, ret), "layer", 0, 0, tiled=True)
    return finish(rows, received, back)


def solution(mesh):
    placed = (P("layer", "slab", None), P("layer", "slab", None), P())
    return jax.shard_map(
        per_device,
        mesh=mesh,
        in_specs=placed,
        out_specs=(P("layer", "slab", None), P("slab", "layer", None)),
        check_vma=False,
    )
```

```python
import jax
import jax.numpy as jnp
from jax import lax
from jax.experimental import pallas as pl
from jax.experimental.pallas import tpu as pltpu
from jax.sharding import PartitionSpec as P

F32 = jnp.float32
LAYERS = 16
ROWS = 16
COLS = 4096
WIDTH = COLS // LAYERS
SLABS = 64
TILE_COLS = 32
PER_TILE = 8
OWNED = 4
EXT_ROWS = 24
EXT_COLS = 384
VMEM_LIMIT = 48 * 1024 * 1024


def lanes():
    return lax.broadcasted_iota(jnp.int32, (8, 128), 1)


def sublanes():
    return lax.broadcasted_iota(jnp.int32, (8, 128), 0)


def pack_kernel(both_ref, owner_ref, out_ref, table_ref):
    lane = lanes()
    zero = jnp.zeros((8, 128), F32)
    table_ref[...] = owner_ref[...]
    for j in range(LAYERS):
        edge = zero
        for q in range(2):
            for g in range(2):
                rows = slice(8 * g, 8 * g + 8)
                base = WIDTH * j
                for t in range(2):
                    out_ref[j, 4 * q + 2 * g + t] = both_ref[q, rows, base + 128 * t : base + 128 * t + 128]
                before = both_ref[q, rows, base - 128 : base] if j > 0 else zero
                after = both_ref[q, rows, base + 256 : base + 384] if j < LAYERS - 1 else zero
                both = jnp.where(lane < 4, after, jnp.where(lane >= 124, before, 0.0))
                edge = edge + pltpu.roll(both, 4 + 8 * (2 * g + q), axis=1)
        out_ref[j, 8] = edge


def halo_kernel(turn_ref, recv_ref, first_ref, second_ref):
    even = turn_ref[0] % 2 == 0

    def put(n, up, down):
        first_ref[n] = jnp.where(even, up, down)
        second_ref[n] = jnp.where(even, down, up)

    lane = lanes()
    sub = sublanes()
    up_edges = [jnp.zeros((8, 128), F32)] * 2
    down_edges = [jnp.zeros((8, 128), F32)] * 2
    for l in range(LAYERS):
        for t in range(2):
            up = jnp.where(sub >= 4, recv_ref[l, 2 + t], pltpu.roll(recv_ref[l, 6 + t], 4, axis=0))
            down = jnp.where(sub < 4, recv_ref[l, t], pltpu.roll(recv_ref[l, 4 + t], 4, axis=0))
            put(2 * l + t, up, down)
        edge = recv_ref[l, 8]
        half, place = l // 8, 16 * (l % 8)
        here = (lane >= place) & (lane < place + 16)
        up_edges[half] = jnp.where(here, pltpu.roll(edge, (place + 112) % 128, axis=1), up_edges[half])
        down_edges[half] = jnp.where(here, pltpu.roll(edge, place, axis=1), down_edges[half])
    up = jnp.where(sub >= 4, up_edges[0], pltpu.roll(up_edges[1], 4, axis=0))
    down = jnp.where(sub < 4, down_edges[0], pltpu.roll(down_edges[1], 4, axis=0))
    put(32, up, down)


def own(value):
    return value[:ROWS, :WIDTH]


def folded(value):
    return (value[:8, :128] + value[8:, :128]) + (value[:8, 128:] + value[8:, 128:])


def krylov_kernel(
    turn_ref, recv_ref, first_ref, second_ref, msg_ref, ret_ref, k_ref, v0_ref, v1_ref, v2_ref, inv_ref, cc_ref, cr_ref, cz_ref, square_ref
):
    lane = lanes()
    sub = sublanes()
    rim = (lane < 4) | (lane >= 124)
    blank = jnp.zeros((EXT_ROWS, EXT_COLS), F32)
    for ref in (k_ref, v0_ref, v1_ref, v2_ref):
        ref[LAYERS] = blank

    def spread(tile, place):
        return jnp.where(rim, pltpu.roll(tile, (252 - place) % 128, axis=1), 0.0)

    even = turn_ref[0] % 2 == 0
    upper = (sub < 4) == even

    def halves(n):
        one, two = first_ref[n], second_ref[n]
        return jnp.where(upper, one, two), pltpu.roll(jnp.where(upper, two, one), 4, axis=0)

    halo_edges = halves(32)
    for l in range(LAYERS):
        edge = recv_ref[l, 8]
        for q, ref in enumerate((k_ref, v0_ref)):
            for g in range(2):
                for t in range(2):
                    ref[l, 8 * g : 8 * g + 8, 128 * t : 128 * t + 128] = recv_ref[l, 4 * q + 2 * g + t]
                ref[l, 8 * g : 8 * g + 8, 256:384] = spread(edge, 8 * (2 * g + q))
            ref[l, 16:24, 256:384] = spread(halo_edges[l // 8], 16 * (l % 8) + 8 * q)
        for t in range(2):
            cols = slice(128 * t, 128 * t + 128)
            k_ref[l, 16:24, cols], v0_ref[l, 16:24, cols] = halves(2 * l + t)

    def setup(l, carry):
        cz_before, s0, m0 = carry
        k = k_ref[l]
        cc = k + pltpu.roll(k, EXT_COLS - 1, axis=1)
        cr = k + pltpu.roll(k, EXT_ROWS - 1, axis=0)
        cz = k + k_ref[l + 1]
        diag = (cc + pltpu.roll(cc, 1, axis=1)) + (cr + pltpu.roll(cr, 1, axis=0)) + (cz + cz_before)
        inv = jnp.where(k > 0.0, 1.0 / diag, 0.0)
        twice = v0_ref[l] * 2.0
        v0 = twice * inv
        cc_ref[l] = cc
        cr_ref[l] = cr
        cz_ref[l] = cz
        inv_ref[l] = inv
        v0_ref[l] = v0
        mine = own(v0)
        for g in range(2):
            for t in range(2):
                ret_ref[l, 2 * g + t] = mine[8 * g : 8 * g + 8, 128 * t : 128 * t + 128]
        return cz, s0 + folded(mine * own(twice)), m0 + mine

    none = jnp.zeros((8, 128), F32)
    no_map = jnp.zeros((ROWS, WIDTH), F32)
    _, s0, m0 = lax.fori_loop(0, LAYERS, setup, (k_ref[0], none, no_map), unroll=8)

    def image(l, v_ref, fz_before):
        v = v_ref[l]
        fc = cc_ref[l] * (v - pltpu.roll(v, EXT_COLS - 1, axis=1))
        fr = cr_ref[l] * (v - pltpu.roll(v, EXT_ROWS - 1, axis=0))
        fz = cz_ref[l] * (v - v_ref[l + 1])
        result = (fc - pltpu.roll(fc, 1, axis=1)) + (fr - pltpu.roll(fr, 1, axis=0)) + (fz - fz_before)
        return v, result, fz

    def step(v_ref, out_ref, slot):
        def body(l, carry):
            fz_before, odd, even, total = carry
            v, result, fz = image(l, v_ref, fz_before)
            after = inv_ref[l] * result
            out_ref[l] = after
            mine = own(after)
            for g in range(2):
                for t in range(2):
                    ret_ref[l, 4 * slot + 2 * g + t] = mine[8 * g : 8 * g + 8, 128 * t : 128 * t + 128]
            got = own(result)
            return fz, odd + folded(own(v) * got), even + folded(mine * got), total + mine

        start = (-(k_ref[0] * v_ref[0]), none, none, no_map)
        return lax.fori_loop(0, LAYERS, body, start, unroll=8)[1:]

    s1, s2, m1 = step(v0_ref, v1_ref, 1)
    s3, s4, m2 = step(v1_ref, v2_ref, 2)

    def last(l, carry):
        fz_before, odd = carry
        v, result, fz = image(l, v2_ref, fz_before)
        return fz, odd + folded(own(v) * own(result))

    _, s5 = lax.fori_loop(0, LAYERS, last, (-(k_ref[0] * v2_ref[0]), none), unroll=8)

    sums = none
    for n, part in enumerate((s0, s1, s2, s3, s4, s5)):
        sums = jnp.where(sub == n, jnp.sum(part), sums)
    first = lax.broadcasted_iota(jnp.int32, (ROWS, 128), 1) % 8 < 4
    for f, total in enumerate((m0, m1, m2)):
        left, right = total[:, :128], total[:, 128:]
        square_ref[16 * f : 16 * f + 16, :] = jnp.where(first, left, pltpu.roll(right, 4, axis=1))
        square_ref[64 + 16 * f : 80 + 16 * f, :] = jnp.where(first, pltpu.roll(left, 124, axis=1), right)
    square_ref[48:56, :] = sums
    square_ref[56:64, :] = none
    square_ref[112:120, :] = none
    square_ref[120:128, :] = none
    turned = square_ref[...].T
    for j in range(LAYERS):
        msg_ref[j] = turned[8 * j : 8 * j + 8, :]


def tree(values):
    while len(values) > 1:
        values = [a + b for a, b in zip(values[::2], values[1::2])]
    return values[0]


def route_kernel(owner_ref, index_ref, recv_ref, msg_ref):
    lane = lax.broadcasted_iota(jnp.int32, (4, 128), 1)
    shared = (lane >= 48) & (lane < 64)
    total = tree([recv_ref[j] for j in range(LAYERS)])
    common = total[:4]
    for o in range(SLABS):
        msg_ref[o] = common
    row = index_ref[0] // PER_TILE
    for c in range(TILE_COLS):
        half = 4 * (c % 2)
        strip = recv_ref[c // 2, half : half + 4]
        msg_ref[owner_ref[row, c]] = jnp.where(shared, common, strip)


def weights(s):
    s0, s1, s2, s3, s4, s5 = s
    a0 = s0 / s1
    z1 = -a0
    n1 = s0 + z1 * (2.0 * s1 + z1 * s2)
    b0 = n1 / s0
    p0, p1 = 1.0 + b0, z1
    a1 = n1 / (p0 * p0 * s1 + p1 * (2.0 * p0 * s2 + p1 * s3))
    x0, x1 = a0 + a1 * p0, a1 * p1
    z1, z2 = z1 - a1 * p0, -(a1 * p1)
    n2 = s0 + z1 * (2.0 * s1 + z1 * s2) + z2 * (2.0 * (s2 + z1 * s3) + z2 * s4)
    b1 = n2 / n1
    p0, p1, p2 = 1.0 + b1 * p0, z1 + b1 * p1, z2
    energy = p0 * p0 * s1 + p1 * (2.0 * p0 * s2 + p1 * s3) + p2 * (2.0 * (p0 * s3 + p1 * s4) + p2 * s5)
    a2 = n2 / energy
    return x0 + a2 * p0, x1 + a2 * p1, a2 * p2


def solved(recv_ref):
    total = tree([recv_ref[s] for s in range(SLABS)])
    return weights([jnp.broadcast_to(total[:1, 48 + n : 49 + n], (8, 128)) for n in range(6)])


def combine_kernel(recv_ref, ret_ref, out_ref):
    w0, w1, w2 = solved(recv_ref)
    for l in range(LAYERS):
        for n in range(4):
            out_ref[l, n] = w0 * ret_ref[l, n] + w1 * ret_ref[l, 4 + n] + w2 * ret_ref[l, 8 + n]


def finish_kernel(rows_ref, recv_ref, back_ref, adjoint_ref, owned_ref):
    lane = lanes()
    sub = sublanes()
    for j in range(LAYERS):
        for n in range(4):
            col = WIDTH * j + 128 * (n % 2)
            adjoint_ref[0, 8 * (n // 2) : 8 * (n // 2) + 8, col : col + 128] = back_ref[j, n]
    w0, w1, w2 = solved(recv_ref)
    for k in range(OWNED):
        row = rows_ref[k]
        tile = jnp.zeros((8, 128), F32)
        for i in range(PER_TILE):
            half = recv_ref[PER_TILE * row + i]
            whole = jnp.concatenate([half, half], axis=0)
            strip = jnp.where(sub < 4, whole, pltpu.roll(whole, 64, axis=1))
            value = w0 * strip + w1 * pltpu.roll(strip, 112, axis=1) + w2 * pltpu.roll(strip, 96, axis=1)
            if i:
                value = pltpu.roll(value, 16 * i, axis=1)
            tile = jnp.where((lane >= 16 * i) & (lane < 16 * i + 16), value, tile)
        owned_ref[k] = tile


VMEM = pl.BlockSpec(memory_space=pltpu.VMEM)
SMEM = pl.BlockSpec(memory_space=pltpu.SMEM)


def shape(*dims):
    return jax.ShapeDtypeStruct(dims, F32)


def call(kernel, ins, outs, scratch=(), interpret=False):
    single = len(outs) == 1
    return pl.pallas_call(
        kernel,
        out_shape=outs[0] if single else tuple(outs),
        in_specs=ins,
        out_specs=VMEM if single else tuple(VMEM for _ in outs),
        scratch_shapes=list(scratch),
        compiler_params=pltpu.CompilerParams(vmem_limit_bytes=VMEM_LIMIT),
        interpret=interpret,
    )


def pack(both, owner, interpret=False):
    outs = [shape(LAYERS, 9, 8, 128), jax.ShapeDtypeStruct(owner.shape, owner.dtype)]
    return call(pack_kernel, [VMEM] * 2, outs, interpret=interpret)(both, owner)


def halo(turn, recv, interpret=False):
    side = shape(2 * LAYERS + 1, 8, 128)
    return call(halo_kernel, [SMEM, VMEM], [side, side], interpret=interpret)(turn, recv)


def krylov(turn, recv, first, second, interpret=False):
    field = pltpu.VMEM((LAYERS + 1, EXT_ROWS, EXT_COLS), F32)
    face = pltpu.VMEM((LAYERS, EXT_ROWS, EXT_COLS), F32)
    return call(
        krylov_kernel,
        [SMEM] + [VMEM] * 3,
        [shape(LAYERS, 8, 128), shape(LAYERS, 12, 8, 128)],
        [field] * 4 + [face] * 4 + [pltpu.VMEM((128, 128), F32)],
        interpret=interpret,
    )(turn, recv, first, second)


def route(owner, index, recv, interpret=False):
    return call(route_kernel, [SMEM, SMEM, VMEM], [shape(SLABS, 4, 128)], interpret=interpret)(owner, index, recv)


def combine(recv, ret, interpret=False):
    return call(combine_kernel, [VMEM] * 2, [shape(LAYERS, 4, 8, 128)], interpret=interpret)(recv, ret)


def finish(rows, recv, back, interpret=False):
    outs = [shape(1, ROWS, COLS), shape(OWNED, 8, 128)]
    return call(finish_kernel, [SMEM, VMEM, VMEM], outs, interpret=interpret)(rows, recv, back)


def owned_rows(tile_owner, index):
    held = jnp.any(tile_owner == index, axis=1)
    rank = jnp.cumsum(held.astype(jnp.int32)) - 1
    slot = jnp.arange(OWNED, dtype=jnp.int32)[:, None]
    row = jnp.arange(tile_owner.shape[0], dtype=jnp.int32)[None, :]
    return jnp.sum(jnp.where(held[None, :] & (rank[None, :] == slot), row, 0), axis=1)


def pairing(turn):
    pairs = []
    for layer in range(LAYERS):
        for low in range((turn + layer) % 2, SLABS - 1, 2):
            here, there = low * LAYERS + layer, (low + 1) * LAYERS + layer
            pairs += [(here, there), (there, here)]
    return pairs


def per_device(adjoint_source, conductivity, tile_owner):
    index = lax.axis_index("slab")
    place = index.reshape(1)
    turn = (index + lax.axis_index("layer")).reshape(1)
    both = jnp.concatenate([conductivity, adjoint_source], axis=0)
    packed, table = pack(both, tile_owner)
    recv = lax.all_to_all(packed, "layer", 0, 0, tiled=True)
    first, second = halo(turn, recv)
    first, table = lax.optimization_barrier((first, table))
    rows = owned_rows(table, index)
    first = lax.ppermute(first, ("slab", "layer"), pairing(0))
    second = lax.ppermute(second, ("slab", "layer"), pairing(1))
    first, second, rows = lax.optimization_barrier((first, second, rows))
    msg, ret = krylov(turn, recv, first, second)
    strips = lax.all_to_all(msg, "layer", 0, 0, tiled=True)
    outgoing = route(table, place, strips)
    received = lax.all_to_all(outgoing, "slab", 0, 0, tiled=True)
    back = lax.all_to_all(combine(received, ret), "layer", 0, 0, tiled=True)
    return finish(rows, received, back)


def solution(mesh):
    placed = (P("layer", "slab", None), P("layer", "slab", None), P())
    return jax.shard_map(
        per_device,
        mesh=mesh,
        in_specs=placed,
        out_specs=(P("layer", "slab", None), P("slab", "layer", None)),
        check_vma=False,
    )
```

```python
import jax
import jax.numpy as jnp
from jax import lax
from jax.experimental import pallas as pl
from jax.experimental.pallas import tpu as pltpu
from jax.sharding import PartitionSpec as P

F32 = jnp.float32
LAYERS = 16
ROWS = 16
COLS = 4096
WIDTH = COLS // LAYERS
SLABS = 64
TILE_COLS = 32
PER_TILE = 8
OWNED = 4
EXT_ROWS = 24
EXT_COLS = 384
VMEM_LIMIT = 48 * 1024 * 1024


def lanes():
    return lax.broadcasted_iota(jnp.int32, (8, 128), 1)


def sublanes():
    return lax.broadcasted_iota(jnp.int32, (8, 128), 0)


def pack_kernel(both_ref, owner_ref, out_ref, table_ref):
    lane = lanes()
    zero = jnp.zeros((8, 128), F32)
    table_ref[...] = owner_ref[...]
    for j in range(LAYERS):
        edge = zero
        for q in range(2):
            for g in range(2):
                rows = slice(8 * g, 8 * g + 8)
                base = WIDTH * j
                for t in range(2):
                    out_ref[j, 4 * q + 2 * g + t] = both_ref[q, rows, base + 128 * t : base + 128 * t + 128]
                before = both_ref[q, rows, base - 128 : base] if j > 0 else zero
                after = both_ref[q, rows, base + 256 : base + 384] if j < LAYERS - 1 else zero
                both = jnp.where(lane < 4, after, jnp.where(lane >= 124, before, 0.0))
                edge = edge + pltpu.roll(both, 4 + 8 * (2 * g + q), axis=1)
        out_ref[j, 8] = edge


def halo_kernel(turn_ref, recv_ref, first_ref, second_ref):
    even = turn_ref[0] % 2 == 0

    def put(n, up, down):
        first_ref[n] = jnp.where(even, up, down)
        second_ref[n] = jnp.where(even, down, up)

    lane = lanes()
    sub = sublanes()
    up_edges = [jnp.zeros((8, 128), F32)] * 2
    down_edges = [jnp.zeros((8, 128), F32)] * 2
    for l in range(LAYERS):
        for t in range(2):
            up = jnp.where(sub >= 4, recv_ref[l, 2 + t], pltpu.roll(recv_ref[l, 6 + t], 4, axis=0))
            down = jnp.where(sub < 4, recv_ref[l, t], pltpu.roll(recv_ref[l, 4 + t], 4, axis=0))
            put(2 * l + t, up, down)
        edge = recv_ref[l, 8]
        half, place = l // 8, 16 * (l % 8)
        here = (lane >= place) & (lane < place + 16)
        up_edges[half] = jnp.where(here, pltpu.roll(edge, (place + 112) % 128, axis=1), up_edges[half])
        down_edges[half] = jnp.where(here, pltpu.roll(edge, place, axis=1), down_edges[half])
    up = jnp.where(sub >= 4, up_edges[0], pltpu.roll(up_edges[1], 4, axis=0))
    down = jnp.where(sub < 4, down_edges[0], pltpu.roll(down_edges[1], 4, axis=0))
    put(32, up, down)


def own(value):
    return value[:ROWS, :WIDTH]


def folded(value):
    return (value[:8, :128] + value[8:, :128]) + (value[:8, 128:] + value[8:, 128:])


def krylov_kernel(
    turn_ref, recv_ref, first_ref, second_ref, msg_ref, ret_ref, k_ref, v0_ref, v1_ref, v2_ref, inv_ref, cc_ref, cr_ref, cz_ref, square_ref
):
    lane = lanes()
    sub = sublanes()
    rim = (lane < 4) | (lane >= 124)
    blank = jnp.zeros((EXT_ROWS, EXT_COLS), F32)
    for ref in (k_ref, v0_ref, v1_ref, v2_ref):
        ref[LAYERS] = blank

    def spread(tile, place):
        return jnp.where(rim, pltpu.roll(tile, (252 - place) % 128, axis=1), 0.0)

    even = turn_ref[0] % 2 == 0
    upper = (sub < 4) == even

    def halves(n):
        one, two = first_ref[n], second_ref[n]
        return jnp.where(upper, one, two), pltpu.roll(jnp.where(upper, two, one), 4, axis=0)

    halo_edges = halves(32)
    for l in range(LAYERS):
        edge = recv_ref[l, 8]
        for q, ref in enumerate((k_ref, v0_ref)):
            for g in range(2):
                for t in range(2):
                    ref[l, 8 * g : 8 * g + 8, 128 * t : 128 * t + 128] = recv_ref[l, 4 * q + 2 * g + t]
                ref[l, 8 * g : 8 * g + 8, 256:384] = spread(edge, 8 * (2 * g + q))
            ref[l, 16:24, 256:384] = spread(halo_edges[l // 8], 16 * (l % 8) + 8 * q)
        for t in range(2):
            cols = slice(128 * t, 128 * t + 128)
            k_ref[l, 16:24, cols], v0_ref[l, 16:24, cols] = halves(2 * l + t)

    def setup(l, carry):
        cz_before, s0, m0 = carry
        k = k_ref[l]
        cc = k + pltpu.roll(k, EXT_COLS - 1, axis=1)
        cr = k + pltpu.roll(k, EXT_ROWS - 1, axis=0)
        cz = k + k_ref[l + 1]
        diag = (cc + pltpu.roll(cc, 1, axis=1)) + (cr + pltpu.roll(cr, 1, axis=0)) + (cz + cz_before)
        inv = jnp.where(k > 0.0, 1.0 / diag, 0.0)
        twice = v0_ref[l] * 2.0
        v0 = twice * inv
        cc_ref[l] = cc
        cr_ref[l] = cr
        cz_ref[l] = cz
        inv_ref[l] = inv
        v0_ref[l] = v0
        mine = own(v0)
        for g in range(2):
            for t in range(2):
                ret_ref[l, 2 * g + t] = mine[8 * g : 8 * g + 8, 128 * t : 128 * t + 128]
        return cz, s0 + folded(mine * own(twice)), m0 + mine

    none = jnp.zeros((8, 128), F32)
    no_map = jnp.zeros((ROWS, WIDTH), F32)
    _, s0, m0 = lax.fori_loop(0, LAYERS, setup, (k_ref[0], none, no_map), unroll=8)

    def image(l, v_ref, fz_before):
        v = v_ref[l]
        fc = cc_ref[l] * (v - pltpu.roll(v, EXT_COLS - 1, axis=1))
        fr = cr_ref[l] * (v - pltpu.roll(v, EXT_ROWS - 1, axis=0))
        fz = cz_ref[l] * (v - v_ref[l + 1])
        result = (fc - pltpu.roll(fc, 1, axis=1)) + (fr - pltpu.roll(fr, 1, axis=0)) + (fz - fz_before)
        return v, result, fz

    def step(v_ref, out_ref, slot):
        def body(l, carry):
            fz_before, odd, even, total = carry
            v, result, fz = image(l, v_ref, fz_before)
            after = inv_ref[l] * result
            out_ref[l] = after
            mine = own(after)
            for g in range(2):
                for t in range(2):
                    ret_ref[l, 4 * slot + 2 * g + t] = mine[8 * g : 8 * g + 8, 128 * t : 128 * t + 128]
            got = own(result)
            return fz, odd + folded(own(v) * got), even + folded(mine * got), total + mine

        start = (-(k_ref[0] * v_ref[0]), none, none, no_map)
        return lax.fori_loop(0, LAYERS, body, start, unroll=8)[1:]

    s1, s2, m1 = step(v0_ref, v1_ref, 1)
    s3, s4, m2 = step(v1_ref, v2_ref, 2)

    def last(l, carry):
        fz_before, odd = carry
        v, result, fz = image(l, v2_ref, fz_before)
        return fz, odd + folded(own(v) * own(result))

    _, s5 = lax.fori_loop(0, LAYERS, last, (-(k_ref[0] * v2_ref[0]), none), unroll=8)

    sums = none
    for n, part in enumerate((s0, s1, s2, s3, s4, s5)):
        sums = jnp.where(sub == n, jnp.sum(part), sums)
    first = lax.broadcasted_iota(jnp.int32, (ROWS, 128), 1) % 8 < 4
    for f, total in enumerate((m0, m1, m2)):
        left, right = total[:, :128], total[:, 128:]
        square_ref[16 * f : 16 * f + 16, :] = jnp.where(first, left, pltpu.roll(right, 4, axis=1))
        square_ref[64 + 16 * f : 80 + 16 * f, :] = jnp.where(first, pltpu.roll(left, 124, axis=1), right)
    square_ref[48:56, :] = sums
    square_ref[56:64, :] = none
    square_ref[112:120, :] = none
    square_ref[120:128, :] = none
    turned = square_ref[...].T
    for j in range(LAYERS):
        msg_ref[j] = turned[8 * j : 8 * j + 8, :]


def tree(values):
    while len(values) > 1:
        values = [a + b for a, b in zip(values[::2], values[1::2])]
    return values[0]


def route_kernel(owner_ref, index_ref, recv_ref, msg_ref):
    lane = lax.broadcasted_iota(jnp.int32, (4, 128), 1)
    shared = (lane >= 48) & (lane < 64)
    total = tree([recv_ref[j] for j in range(LAYERS)])
    common = total[:4]
    for o in range(SLABS):
        msg_ref[o] = common
    row = index_ref[0] // PER_TILE
    for c in range(TILE_COLS):
        half = 4 * (c % 2)
        strip = recv_ref[c // 2, half : half + 4]
        msg_ref[owner_ref[row, c]] = jnp.where(shared, common, strip)


def weights(s):
    s0, s1, s2, s3, s4, s5 = s
    a0 = s0 / s1
    z1 = -a0
    n1 = s0 + z1 * (2.0 * s1 + z1 * s2)
    b0 = n1 / s0
    p0, p1 = 1.0 + b0, z1
    a1 = n1 / (p0 * p0 * s1 + p1 * (2.0 * p0 * s2 + p1 * s3))
    x0, x1 = a0 + a1 * p0, a1 * p1
    z1, z2 = z1 - a1 * p0, -(a1 * p1)
    n2 = s0 + z1 * (2.0 * s1 + z1 * s2) + z2 * (2.0 * (s2 + z1 * s3) + z2 * s4)
    b1 = n2 / n1
    p0, p1, p2 = 1.0 + b1 * p0, z1 + b1 * p1, z2
    energy = p0 * p0 * s1 + p1 * (2.0 * p0 * s2 + p1 * s3) + p2 * (2.0 * (p0 * s3 + p1 * s4) + p2 * s5)
    a2 = n2 / energy
    return x0 + a2 * p0, x1 + a2 * p1, a2 * p2


def solved(recv_ref):
    total = tree([recv_ref[s] for s in range(SLABS)])
    return weights([jnp.broadcast_to(total[:1, 48 + n : 49 + n], (8, 128)) for n in range(6)])


def combine_kernel(recv_ref, ret_ref, out_ref):
    w0, w1, w2 = solved(recv_ref)
    for l in range(LAYERS):
        for n in range(4):
            out_ref[l, n] = w0 * ret_ref[l, n] + w1 * ret_ref[l, 4 + n] + w2 * ret_ref[l, 8 + n]


def finish_kernel(rows_ref, recv_ref, back_ref, adjoint_ref, owned_ref):
    lane = lanes()
    sub = sublanes()
    for j in range(LAYERS):
        for n in range(4):
            col = WIDTH * j + 128 * (n % 2)
            adjoint_ref[0, 8 * (n // 2) : 8 * (n // 2) + 8, col : col + 128] = back_ref[j, n]
    w0, w1, w2 = solved(recv_ref)
    for k in range(OWNED):
        row = rows_ref[k]
        tile = jnp.zeros((8, 128), F32)
        for i in range(PER_TILE):
            half = recv_ref[PER_TILE * row + i]
            whole = jnp.concatenate([half, half], axis=0)
            strip = jnp.where(sub < 4, whole, pltpu.roll(whole, 64, axis=1))
            value = w0 * strip + w1 * pltpu.roll(strip, 112, axis=1) + w2 * pltpu.roll(strip, 96, axis=1)
            if i:
                value = pltpu.roll(value, 16 * i, axis=1)
            tile = jnp.where((lane >= 16 * i) & (lane < 16 * i + 16), value, tile)
        owned_ref[k] = tile


VMEM = pl.BlockSpec(memory_space=pltpu.VMEM)
SMEM = pl.BlockSpec(memory_space=pltpu.SMEM)


def shape(*dims):
    return jax.ShapeDtypeStruct(dims, F32)


def call(kernel, ins, outs, scratch=(), interpret=False):
    single = len(outs) == 1
    return pl.pallas_call(
        kernel,
        out_shape=outs[0] if single else tuple(outs),
        in_specs=ins,
        out_specs=VMEM if single else tuple(VMEM for _ in outs),
        scratch_shapes=list(scratch),
        compiler_params=pltpu.CompilerParams(vmem_limit_bytes=VMEM_LIMIT),
        interpret=interpret,
    )


def pack(both, owner, interpret=False):
    outs = [shape(LAYERS, 9, 8, 128), jax.ShapeDtypeStruct(owner.shape, owner.dtype)]
    return call(pack_kernel, [VMEM] * 2, outs, interpret=interpret)(both, owner)


def halo(turn, recv, interpret=False):
    side = shape(2 * LAYERS + 1, 8, 128)
    return call(halo_kernel, [SMEM, VMEM], [side, side], interpret=interpret)(turn, recv)


def krylov(turn, recv, first, second, interpret=False):
    field = pltpu.VMEM((LAYERS + 1, EXT_ROWS, EXT_COLS), F32)
    face = pltpu.VMEM((LAYERS, EXT_ROWS, EXT_COLS), F32)
    return call(
        krylov_kernel,
        [SMEM] + [VMEM] * 3,
        [shape(LAYERS, 8, 128), shape(LAYERS, 12, 8, 128)],
        [field] * 4 + [face] * 4 + [pltpu.VMEM((128, 128), F32)],
        interpret=interpret,
    )(turn, recv, first, second)


def route(owner, index, recv, interpret=False):
    return call(route_kernel, [SMEM, SMEM, VMEM], [shape(SLABS, 4, 128)], interpret=interpret)(owner, index, recv)


def combine(recv, ret, interpret=False):
    return call(combine_kernel, [VMEM] * 2, [shape(LAYERS, 4, 8, 128)], interpret=interpret)(recv, ret)


def finish(rows, recv, back, interpret=False):
    outs = [shape(1, ROWS, COLS), shape(OWNED, 8, 128)]
    return call(finish_kernel, [SMEM, VMEM, VMEM], outs, interpret=interpret)(rows, recv, back)


def owned_rows(tile_owner, index):
    held = jnp.any(tile_owner == index, axis=1)
    rank = jnp.cumsum(held.astype(jnp.int32)) - 1
    slot = jnp.arange(OWNED, dtype=jnp.int32)[:, None]
    row = jnp.arange(tile_owner.shape[0], dtype=jnp.int32)[None, :]
    return jnp.sum(jnp.where(held[None, :] & (rank[None, :] == slot), row, 0), axis=1)


def pairing(first):
    pairs = [(low, low + 1) for low in range(first, SLABS - 1, 2)]
    return pairs + [(high, low) for low, high in pairs]


def per_device(adjoint_source, conductivity, tile_owner):
    index = lax.axis_index("slab")
    place = index.reshape(1)
    turn = (index + 1).reshape(1)
    both = jnp.concatenate([conductivity, adjoint_source], axis=0)
    packed, table = pack(both, tile_owner)
    recv = lax.all_to_all(packed, "layer", 0, 0, tiled=True)
    first, second = halo(turn, recv)
    first, table = lax.optimization_barrier((first, table))
    rows = owned_rows(table, index)
    first = lax.ppermute(first, "slab", pairing(1))
    second = lax.ppermute(second, "slab", pairing(0))
    first, second, rows = lax.optimization_barrier((first, second, rows))
    msg, ret = krylov(turn, recv, first, second)
    strips = lax.all_to_all(msg, "layer", 0, 0, tiled=True)
    outgoing = route(table, place, strips)
    received = lax.all_to_all(outgoing, "slab", 0, 0, tiled=True)
    back = lax.all_to_all(combine(received, ret), "layer", 0, 0, tiled=True)
    return finish(rows, received, back)


def solution(mesh):
    placed = (P("layer", "slab", None), P("layer", "slab", None), P())
    return jax.shard_map(
        per_device,
        mesh=mesh,
        in_specs=placed,
        out_specs=(P("layer", "slab", None), P("slab", "layer", None)),
        check_vma=False,
    )
```

```python
import jax
import jax.numpy as jnp
from jax import lax
from jax.experimental import pallas as pl
from jax.experimental.pallas import tpu as pltpu
from jax.sharding import PartitionSpec as P

F32 = jnp.float32
LAYERS = 16
ROWS = 16
COLS = 4096
WIDTH = COLS // LAYERS
SLABS = 64
TILE_COLS = 32
PER_TILE = 8
OWNED = 4
EXT_ROWS = 24
EXT_COLS = 384
SCALE = 2.0**-6
VMEM_LIMIT = 48 * 1024 * 1024


def lanes():
    return lax.broadcasted_iota(jnp.int32, (8, 128), 1)


def sublanes():
    return lax.broadcasted_iota(jnp.int32, (8, 128), 0)


def pack_kernel(both_ref, owner_ref, out_ref, table_ref):
    lane = lanes()
    zero = jnp.zeros((8, 128), F32)
    table_ref[...] = owner_ref[...]
    for j in range(LAYERS):
        edge = zero
        for q in range(2):
            for g in range(2):
                rows = slice(8 * g, 8 * g + 8)
                base = WIDTH * j
                for t in range(2):
                    out_ref[j, 4 * q + 2 * g + t] = both_ref[q, rows, base + 128 * t : base + 128 * t + 128]
                before = both_ref[q, rows, base - 128 : base] if j > 0 else zero
                after = both_ref[q, rows, base + 256 : base + 384] if j < LAYERS - 1 else zero
                both = jnp.where(lane < 4, after, jnp.where(lane >= 124, before, 0.0))
                edge = edge + pltpu.roll(both, 4 + 8 * (2 * g + q), axis=1)
        out_ref[j, 8] = edge


def halo_kernel(turn_ref, recv_ref, first_ref, second_ref):
    even = turn_ref[0] % 2 == 0

    def put(n, up, down):
        first_ref[n] = jnp.where(even, up, down)
        second_ref[n] = jnp.where(even, down, up)

    lane = lanes()
    sub = sublanes()
    up_edges = [jnp.zeros((8, 128), F32)] * 2
    down_edges = [jnp.zeros((8, 128), F32)] * 2
    for l in range(LAYERS):
        for t in range(2):
            up = jnp.where(sub >= 4, recv_ref[l, 2 + t], pltpu.roll(recv_ref[l, 6 + t], 4, axis=0))
            down = jnp.where(sub < 4, recv_ref[l, t], pltpu.roll(recv_ref[l, 4 + t], 4, axis=0))
            put(2 * l + t, up, down)
        edge = recv_ref[l, 8]
        half, place = l // 8, 16 * (l % 8)
        here = (lane >= place) & (lane < place + 16)
        up_edges[half] = jnp.where(here, pltpu.roll(edge, (place + 112) % 128, axis=1), up_edges[half])
        down_edges[half] = jnp.where(here, pltpu.roll(edge, place, axis=1), down_edges[half])
    up = jnp.where(sub >= 4, up_edges[0], pltpu.roll(up_edges[1], 4, axis=0))
    down = jnp.where(sub < 4, down_edges[0], pltpu.roll(down_edges[1], 4, axis=0))
    put(32, up, down)


def own(value):
    return value[:ROWS, :WIDTH]


def folded(value):
    return (value[:8, :128] + value[8:, :128]) + (value[:8, 128:] + value[8:, 128:])


def krylov_kernel(
    turn_ref, recv_ref, first_ref, second_ref, msg_ref, ret_ref, k_ref, v0_ref, v1_ref, v2_ref, inv_ref, cc_ref, cr_ref, cz_ref, square_ref
):
    lane = lanes()
    sub = sublanes()
    rim = (lane < 4) | (lane >= 124)
    blank = jnp.zeros((EXT_ROWS, EXT_COLS), F32)
    for ref in (k_ref, v0_ref, v1_ref, v2_ref):
        ref[LAYERS] = blank

    def spread(tile, place):
        return jnp.where(rim, pltpu.roll(tile, (252 - place) % 128, axis=1), 0.0)

    even = turn_ref[0] % 2 == 0
    upper = (sub < 4) == even

    def halves(n):
        one, two = first_ref[n], second_ref[n]
        return jnp.where(upper, one, two), pltpu.roll(jnp.where(upper, two, one), 4, axis=0)

    halo_edges = halves(32)
    for l in range(LAYERS):
        edge = recv_ref[l, 8]
        for q, ref in enumerate((k_ref, v0_ref)):
            for g in range(2):
                for t in range(2):
                    ref[l, 8 * g : 8 * g + 8, 128 * t : 128 * t + 128] = recv_ref[l, 4 * q + 2 * g + t]
                ref[l, 8 * g : 8 * g + 8, 256:384] = spread(edge, 8 * (2 * g + q))
            ref[l, 16:24, 256:384] = spread(halo_edges[l // 8], 16 * (l % 8) + 8 * q)
        for t in range(2):
            cols = slice(128 * t, 128 * t + 128)
            k_ref[l, 16:24, cols], v0_ref[l, 16:24, cols] = halves(2 * l + t)

    def setup(l, carry):
        cz_before, s0, m0 = carry
        k = k_ref[l]
        cc = k + pltpu.roll(k, EXT_COLS - 1, axis=1)
        cr = k + pltpu.roll(k, EXT_ROWS - 1, axis=0)
        cz = k + k_ref[l + 1]
        diag = (cc + pltpu.roll(cc, 1, axis=1)) + (cr + pltpu.roll(cr, 1, axis=0)) + (cz + cz_before)
        inv = jnp.where(k > 0.0, 1.0 / diag, 0.0)
        twice = v0_ref[l] * 2.0
        v0 = twice * inv
        cc_ref[l] = cc
        cr_ref[l] = cr
        cz_ref[l] = cz
        inv_ref[l] = inv
        v0_ref[l] = v0
        mine = own(v0)
        for g in range(2):
            for t in range(2):
                ret_ref[l, 2 * g + t] = mine[8 * g : 8 * g + 8, 128 * t : 128 * t + 128]
        return cz, s0 + folded(mine * (own(twice) * SCALE)), m0 + mine

    none = jnp.zeros((8, 128), F32)
    no_map = jnp.zeros((ROWS, WIDTH), F32)
    _, s0, m0 = lax.fori_loop(0, LAYERS, setup, (k_ref[0], none, no_map), unroll=8)

    def image(l, v_ref, fz_before):
        v = v_ref[l]
        fc = cc_ref[l] * (v - pltpu.roll(v, EXT_COLS - 1, axis=1))
        fr = cr_ref[l] * (v - pltpu.roll(v, EXT_ROWS - 1, axis=0))
        fz = cz_ref[l] * (v - v_ref[l + 1])
        result = (fc - pltpu.roll(fc, 1, axis=1)) + (fr - pltpu.roll(fr, 1, axis=0)) + (fz - fz_before)
        return v, result, fz

    def step(v_ref, out_ref, slot):
        def body(l, carry):
            fz_before, odd, even, total = carry
            v, result, fz = image(l, v_ref, fz_before)
            after = inv_ref[l] * result
            out_ref[l] = after
            mine = own(after)
            for g in range(2):
                for t in range(2):
                    ret_ref[l, 4 * slot + 2 * g + t] = mine[8 * g : 8 * g + 8, 128 * t : 128 * t + 128]
            got = own(result) * SCALE
            return fz, odd + folded(own(v) * got), even + folded(mine * got), total + mine

        start = (-(k_ref[0] * v_ref[0]), none, none, no_map)
        return lax.fori_loop(0, LAYERS, body, start, unroll=8)[1:]

    s1, s2, m1 = step(v0_ref, v1_ref, 1)
    s3, s4, m2 = step(v1_ref, v2_ref, 2)

    def last(l, carry):
        fz_before, odd = carry
        v, result, fz = image(l, v2_ref, fz_before)
        return fz, odd + folded(own(v) * (own(result) * SCALE))

    _, s5 = lax.fori_loop(0, LAYERS, last, (-(k_ref[0] * v2_ref[0]), none), unroll=16)

    sums = none
    for n, part in enumerate((s0, s1, s2, s3, s4, s5)):
        sums = jnp.where(sub == n, jnp.sum(part), sums)
    first = lax.broadcasted_iota(jnp.int32, (ROWS, 128), 1) % 8 < 4
    for f, total in enumerate((m0, m1, m2)):
        left, right = total[:, :128], total[:, 128:]
        square_ref[16 * f : 16 * f + 16, :] = jnp.where(first, left, pltpu.roll(right, 4, axis=1))
        square_ref[64 + 16 * f : 80 + 16 * f, :] = jnp.where(first, pltpu.roll(left, 124, axis=1), right)
    square_ref[48:56, :] = sums
    square_ref[56:64, :] = none
    square_ref[112:120, :] = none
    square_ref[120:128, :] = none
    turned = square_ref[...].T
    for j in range(LAYERS):
        msg_ref[j] = turned[8 * j : 8 * j + 8, :]


def tree(values):
    while len(values) > 1:
        values = [a + b for a, b in zip(values[::2], values[1::2])]
    return values[0]


def route_kernel(owner_ref, index_ref, recv_ref, msg_ref):
    lane = lax.broadcasted_iota(jnp.int32, (4, 128), 1)
    shared = (lane >= 48) & (lane < 64)
    total = tree([recv_ref[j] for j in range(LAYERS)])
    common = total[:4]
    for o in range(SLABS):
        msg_ref[o] = common
    row = index_ref[0] // PER_TILE
    for c in range(TILE_COLS):
        half = 4 * (c % 2)
        strip = recv_ref[c // 2, half : half + 4]
        msg_ref[owner_ref[row, c]] = jnp.where(shared, common, strip)


def weights(s):
    level = jnp.where(s[0] > 2.0**60, 2.0**-60, jnp.where(s[0] < 2.0**-60, 2.0**60, 1.0))
    s0, s1, s2, s3, s4, s5 = [value * level for value in s]
    a0 = s0 / s1
    z1 = -a0
    n1 = s0 + z1 * (2.0 * s1 + z1 * s2)
    b0 = n1 / s0
    p0, p1 = 1.0 + b0, z1
    a1 = n1 / (p0 * p0 * s1 + p1 * (2.0 * p0 * s2 + p1 * s3))
    x0, x1 = a0 + a1 * p0, a1 * p1
    z1, z2 = z1 - a1 * p0, -(a1 * p1)
    n2 = s0 + z1 * (2.0 * s1 + z1 * s2) + z2 * (2.0 * (s2 + z1 * s3) + z2 * s4)
    b1 = n2 / n1
    p0, p1, p2 = 1.0 + b1 * p0, z1 + b1 * p1, z2
    energy = p0 * p0 * s1 + p1 * (2.0 * p0 * s2 + p1 * s3) + p2 * (2.0 * (p0 * s3 + p1 * s4) + p2 * s5)
    a2 = n2 / energy
    return x0 + a2 * p0, x1 + a2 * p1, a2 * p2


def solved(recv_ref):
    total = tree([recv_ref[s] for s in range(SLABS)])
    return weights([jnp.broadcast_to(total[:1, 48 + n : 49 + n], (8, 128)) for n in range(6)])


def combine_kernel(recv_ref, ret_ref, out_ref):
    w0, w1, w2 = solved(recv_ref)
    for l in range(LAYERS):
        for n in range(4):
            out_ref[l, n] = w0 * ret_ref[l, n] + w1 * ret_ref[l, 4 + n] + w2 * ret_ref[l, 8 + n]


def finish_kernel(rows_ref, recv_ref, back_ref, adjoint_ref, owned_ref):
    lane = lanes()
    sub = sublanes()
    for j in range(LAYERS):
        for n in range(4):
            col = WIDTH * j + 128 * (n % 2)
            adjoint_ref[0, 8 * (n // 2) : 8 * (n // 2) + 8, col : col + 128] = back_ref[j, n]
    w0, w1, w2 = solved(recv_ref)
    for k in range(OWNED):
        row = rows_ref[k]
        tile = jnp.zeros((8, 128), F32)
        for i in range(PER_TILE):
            half = recv_ref[PER_TILE * row + i]
            whole = jnp.concatenate([half, half], axis=0)
            strip = jnp.where(sub < 4, whole, pltpu.roll(whole, 64, axis=1))
            value = w0 * strip + w1 * pltpu.roll(strip, 112, axis=1) + w2 * pltpu.roll(strip, 96, axis=1)
            if i:
                value = pltpu.roll(value, 16 * i, axis=1)
            tile = jnp.where((lane >= 16 * i) & (lane < 16 * i + 16), value, tile)
        owned_ref[k] = tile


VMEM = pl.BlockSpec(memory_space=pltpu.VMEM)
SMEM = pl.BlockSpec(memory_space=pltpu.SMEM)


def shape(*dims):
    return jax.ShapeDtypeStruct(dims, F32)


def call(kernel, ins, outs, scratch=(), interpret=False):
    single = len(outs) == 1
    return pl.pallas_call(
        kernel,
        out_shape=outs[0] if single else tuple(outs),
        in_specs=ins,
        out_specs=VMEM if single else tuple(VMEM for _ in outs),
        scratch_shapes=list(scratch),
        compiler_params=pltpu.CompilerParams(vmem_limit_bytes=VMEM_LIMIT),
        interpret=interpret,
    )


def pack(both, owner, interpret=False):
    outs = [shape(LAYERS, 9, 8, 128), jax.ShapeDtypeStruct(owner.shape, owner.dtype)]
    return call(pack_kernel, [VMEM] * 2, outs, interpret=interpret)(both, owner)


def halo(turn, recv, interpret=False):
    side = shape(2 * LAYERS + 1, 8, 128)
    return call(halo_kernel, [SMEM, VMEM], [side, side], interpret=interpret)(turn, recv)


def krylov(turn, recv, first, second, interpret=False):
    field = pltpu.VMEM((LAYERS + 1, EXT_ROWS, EXT_COLS), F32)
    face = pltpu.VMEM((LAYERS, EXT_ROWS, EXT_COLS), F32)
    return call(
        krylov_kernel,
        [SMEM] + [VMEM] * 3,
        [shape(LAYERS, 8, 128), shape(LAYERS, 12, 8, 128)],
        [field] * 4 + [face] * 4 + [pltpu.VMEM((128, 128), F32)],
        interpret=interpret,
    )(turn, recv, first, second)


def route(owner, index, recv, interpret=False):
    return call(route_kernel, [SMEM, SMEM, VMEM], [shape(SLABS, 4, 128)], interpret=interpret)(owner, index, recv)


def combine(recv, ret, interpret=False):
    return call(combine_kernel, [VMEM] * 2, [shape(LAYERS, 4, 8, 128)], interpret=interpret)(recv, ret)


def finish(rows, recv, back, interpret=False):
    outs = [shape(1, ROWS, COLS), shape(OWNED, 8, 128)]
    return call(finish_kernel, [SMEM, VMEM, VMEM], outs, interpret=interpret)(rows, recv, back)


def owned_rows(tile_owner, index):
    held = jnp.any(tile_owner == index, axis=1)
    rank = jnp.cumsum(held.astype(jnp.int32)) - 1
    slot = jnp.arange(OWNED, dtype=jnp.int32)[:, None]
    row = jnp.arange(tile_owner.shape[0], dtype=jnp.int32)[None, :]
    return jnp.sum(jnp.where(held[None, :] & (rank[None, :] == slot), row, 0), axis=1)


def pairing(first):
    pairs = [(low, low + 1) for low in range(first, SLABS - 1, 2)]
    return pairs + [(high, low) for low, high in pairs]


def per_device(adjoint_source, conductivity, tile_owner):
    index = lax.axis_index("slab")
    place = index.reshape(1)
    turn = (index + 1).reshape(1)
    both = jnp.concatenate([conductivity, adjoint_source], axis=0)
    packed, table = pack(both, tile_owner)
    recv = lax.all_to_all(packed, "layer", 0, 0, tiled=True)
    first, second = halo(turn, recv)
    first, table = lax.optimization_barrier((first, table))
    rows = owned_rows(table, index)
    first = lax.ppermute(first, "slab", pairing(1))
    second = lax.ppermute(second, "slab", pairing(0))
    first, second, rows = lax.optimization_barrier((first, second, rows))
    msg, ret = krylov(turn, recv, first, second)
    strips = lax.all_to_all(msg, "layer", 0, 0, tiled=True)
    outgoing = route(table, place, strips)
    received = lax.all_to_all(outgoing, "slab", 0, 0, tiled=True)
    back = lax.all_to_all(combine(received, ret), "layer", 0, 0, tiled=True)
    return finish(rows, received, back)


def solution(mesh):
    placed = (P("layer", "slab", None), P("layer", "slab", None), P())
    return jax.shard_map(
        per_device,
        mesh=mesh,
        in_specs=placed,
        out_specs=(P("layer", "slab", None), P("slab", "layer", None)),
        check_vma=False,
    )
```

```python
import jax
import jax.numpy as jnp
from jax import lax
from jax.experimental import pallas as pl
from jax.experimental.pallas import tpu as pltpu
from jax.sharding import PartitionSpec as P

F32 = jnp.float32
LAYERS = 16
ROWS = 16
COLS = 4096
WIDTH = COLS // LAYERS
SLABS = 64
TILE_COLS = 32
PER_TILE = 8
OWNED = 4
EXT_ROWS = 24
EXT_COLS = 384
SCALE = 2.0**-6
VMEM_LIMIT = 48 * 1024 * 1024


def lanes():
    return lax.broadcasted_iota(jnp.int32, (8, 128), 1)


def sublanes():
    return lax.broadcasted_iota(jnp.int32, (8, 128), 0)


def pack_kernel(both_ref, owner_ref, out_ref, table_ref):
    lane = lanes()
    zero = jnp.zeros((8, 128), F32)
    table_ref[...] = owner_ref[...]
    for j in range(LAYERS):
        edge = zero
        for q in range(2):
            for g in range(2):
                rows = slice(8 * g, 8 * g + 8)
                base = WIDTH * j
                for t in range(2):
                    out_ref[j, 4 * q + 2 * g + t] = both_ref[q, rows, base + 128 * t : base + 128 * t + 128]
                before = both_ref[q, rows, base - 128 : base] if j > 0 else zero
                after = both_ref[q, rows, base + 256 : base + 384] if j < LAYERS - 1 else zero
                both = jnp.where(lane < 4, after, jnp.where(lane >= 124, before, 0.0))
                edge = edge + pltpu.roll(both, 4 + 8 * (2 * g + q), axis=1)
        out_ref[j, 8] = edge


def halo_kernel(turn_ref, recv_ref, first_ref, second_ref):
    even = turn_ref[0] % 2 == 0

    def put(n, up, down):
        first_ref[n] = jnp.where(even, up, down)
        second_ref[n] = jnp.where(even, down, up)

    lane = lanes()
    sub = sublanes()
    up_edges = [jnp.zeros((8, 128), F32)] * 2
    down_edges = [jnp.zeros((8, 128), F32)] * 2
    for l in range(LAYERS):
        for t in range(2):
            up = jnp.where(sub >= 4, recv_ref[l, 2 + t], pltpu.roll(recv_ref[l, 6 + t], 4, axis=0))
            down = jnp.where(sub < 4, recv_ref[l, t], pltpu.roll(recv_ref[l, 4 + t], 4, axis=0))
            put(2 * l + t, up, down)
        edge = recv_ref[l, 8]
        half, place = l // 8, 16 * (l % 8)
        here = (lane >= place) & (lane < place + 16)
        up_edges[half] = jnp.where(here, pltpu.roll(edge, (place + 112) % 128, axis=1), up_edges[half])
        down_edges[half] = jnp.where(here, pltpu.roll(edge, place, axis=1), down_edges[half])
    up = jnp.where(sub >= 4, up_edges[0], pltpu.roll(up_edges[1], 4, axis=0))
    down = jnp.where(sub < 4, down_edges[0], pltpu.roll(down_edges[1], 4, axis=0))
    put(32, up, down)


def own(value):
    return value[:ROWS, :WIDTH]


def folded(value):
    return (value[:8, :128] + value[8:, :128]) + (value[:8, 128:] + value[8:, 128:])


def spread(tile, place):
    lane = lanes()
    return jnp.where((lane < 4) | (lane >= 124), pltpu.roll(tile, (252 - place) % 128, axis=1), 0.0)


def stage_kernel(recv_ref, k_ref, s_ref, cc_ref, cz_ref, diag_ref):
    k_ref[LAYERS] = jnp.zeros((ROWS, EXT_COLS), F32)
    for l in range(LAYERS):
        edge = recv_ref[l, 8]
        for q, ref in enumerate((k_ref, s_ref)):
            for g in range(2):
                rows = slice(8 * g, 8 * g + 8)
                for t in range(2):
                    ref[l, rows, 128 * t : 128 * t + 128] = recv_ref[l, 4 * q + 2 * g + t]
                ref[l, rows, 256:384] = spread(edge, 8 * (2 * g + q))

    def body(l, cz_before):
        k = k_ref[l]
        cc = k + pltpu.roll(k, EXT_COLS - 1, axis=1)
        cz = k + k_ref[l + 1]
        cc_ref[l] = cc
        cz_ref[l] = cz
        diag_ref[l] = (cc + pltpu.roll(cc, 1, axis=1)) + (cz + cz_before)
        return cz

    lax.fori_loop(0, LAYERS, body, k_ref[0], unroll=8)


def krylov_kernel(
    turn_ref, first_ref, second_ref, own_k_ref, own_s_ref, own_cc_ref, own_cz_ref, own_diag_ref, msg_ref, ret_ref,
    k_ref, v0_ref, v1_ref, v2_ref, inv_ref, cc_ref, cr_ref, cz_ref, square_ref
):
    sub = sublanes()
    blank = jnp.zeros((EXT_ROWS, EXT_COLS), F32)
    k_ref[LAYERS] = blank[ROWS:]
    for ref in (v0_ref, v1_ref, v2_ref):
        ref[LAYERS] = blank

    even = turn_ref[0] % 2 == 0
    upper = (sub < 4) == even

    def halves(n):
        one, two = first_ref[n], second_ref[n]
        return jnp.where(upper, one, two), pltpu.roll(jnp.where(upper, two, one), 4, axis=0)

    halo_edges = halves(32)
    for l in range(LAYERS):
        place = 16 * (l % 8)
        k_ref[l, :, 256:384] = spread(halo_edges[l // 8], place)
        v0_ref[l, 16:24, 256:384] = spread(halo_edges[l // 8], place + 8)
        for t in range(2):
            cols = slice(128 * t, 128 * t + 128)
            k_ref[l, :, cols], v0_ref[l, 16:24, cols] = halves(2 * l + t)

    def joined(own_ref, rim_ref, l):
        return jnp.concatenate([own_ref[l], rim_ref[l]], axis=0)

    def setup(l, carry):
        cz_before, s0, m0 = carry
        rim = k_ref[l]
        cc = rim + pltpu.roll(rim, EXT_COLS - 1, axis=1)
        cz = rim + k_ref[l + 1]
        cc_ref[l] = cc
        cz_ref[l] = cz
        diag = (cc + pltpu.roll(cc, 1, axis=1)) + (cz + cz_before)
        k = joined(own_k_ref, k_ref, l)
        cr = k + pltpu.roll(k, EXT_ROWS - 1, axis=0)
        cr_ref[l] = cr
        diag = jnp.concatenate([own_diag_ref[l], diag], axis=0) + (cr + pltpu.roll(cr, 1, axis=0))
        inv = jnp.where(k > 0.0, 1.0 / diag, 0.0)
        twice = jnp.concatenate([own_s_ref[l], v0_ref[l, 16:24, :]], axis=0) * 2.0
        v0 = twice * inv
        inv_ref[l] = inv
        v0_ref[l] = v0
        mine = own(v0)
        for g in range(2):
            for t in range(2):
                ret_ref[l, 2 * g + t] = mine[8 * g : 8 * g + 8, 128 * t : 128 * t + 128]
        return cz, s0 + folded(mine * (own(twice) * SCALE)), m0 + mine

    none = jnp.zeros((8, 128), F32)
    no_map = jnp.zeros((ROWS, WIDTH), F32)
    _, s0, m0 = lax.fori_loop(0, LAYERS, setup, (k_ref[0], none, no_map), unroll=8)

    def image(l, v_ref, fz_before):
        v = v_ref[l]
        fc = joined(own_cc_ref, cc_ref, l) * (v - pltpu.roll(v, EXT_COLS - 1, axis=1))
        fr = cr_ref[l] * (v - pltpu.roll(v, EXT_ROWS - 1, axis=0))
        fz = joined(own_cz_ref, cz_ref, l) * (v - v_ref[l + 1])
        result = (fc - pltpu.roll(fc, 1, axis=1)) + (fr - pltpu.roll(fr, 1, axis=0)) + (fz - fz_before)
        return v, result, fz

    def step(v_ref, out_ref, slot):
        def body(l, carry):
            fz_before, odd, even, total = carry
            v, result, fz = image(l, v_ref, fz_before)
            after = inv_ref[l] * result
            out_ref[l] = after
            mine = own(after)
            for g in range(2):
                for t in range(2):
                    ret_ref[l, 4 * slot + 2 * g + t] = mine[8 * g : 8 * g + 8, 128 * t : 128 * t + 128]
            got = own(result) * SCALE
            return fz, odd + folded(own(v) * got), even + folded(mine * got), total + mine

        start = (-(joined(own_k_ref, k_ref, 0) * v_ref[0]), none, none, no_map)
        return lax.fori_loop(0, LAYERS, body, start, unroll=8)[1:]

    s1, s2, m1 = step(v0_ref, v1_ref, 1)
    s3, s4, m2 = step(v1_ref, v2_ref, 2)

    def last(l, carry):
        fz_before, odd = carry
        v, result, fz = image(l, v2_ref, fz_before)
        return fz, odd + folded(own(v) * (own(result) * SCALE))

    _, s5 = lax.fori_loop(0, LAYERS, last, (-(joined(own_k_ref, k_ref, 0) * v2_ref[0]), none), unroll=16)

    sums = none
    for n, part in enumerate((s0, s1, s2, s3, s4, s5)):
        sums = jnp.where(sub == n, jnp.sum(part), sums)
    first = lax.broadcasted_iota(jnp.int32, (ROWS, 128), 1) % 8 < 4
    for f, total in enumerate((m0, m1, m2)):
        left, right = total[:, :128], total[:, 128:]
        square_ref[16 * f : 16 * f + 16, :] = jnp.where(first, left, pltpu.roll(right, 4, axis=1))
        square_ref[64 + 16 * f : 80 + 16 * f, :] = jnp.where(first, pltpu.roll(left, 124, axis=1), right)
    square_ref[48:56, :] = sums
    square_ref[56:64, :] = none
    square_ref[112:120, :] = none
    square_ref[120:128, :] = none
    turned = square_ref[...].T
    for j in range(LAYERS):
        msg_ref[j] = turned[8 * j : 8 * j + 8, :]


def tree(values):
    while len(values) > 1:
        values = [a + b for a, b in zip(values[::2], values[1::2])]
    return values[0]


def route_kernel(owner_ref, index_ref, recv_ref, msg_ref):
    lane = lax.broadcasted_iota(jnp.int32, (4, 128), 1)
    shared = (lane >= 48) & (lane < 64)
    total = tree([recv_ref[j] for j in range(LAYERS)])
    common = total[:4]
    for o in range(SLABS):
        msg_ref[o] = common
    row = index_ref[0] // PER_TILE
    for c in range(TILE_COLS):
        half = 4 * (c % 2)
        strip = recv_ref[c // 2, half : half + 4]
        msg_ref[owner_ref[row, c]] = jnp.where(shared, common, strip)


def weights(s):
    level = jnp.where(s[0] > 2.0**60, 2.0**-60, jnp.where(s[0] < 2.0**-60, 2.0**60, 1.0))
    s0, s1, s2, s3, s4, s5 = [value * level for value in s]
    a0 = s0 / s1
    z1 = -a0
    n1 = s0 + z1 * (2.0 * s1 + z1 * s2)
    b0 = n1 / s0
    p0, p1 = 1.0 + b0, z1
    a1 = n1 / (p0 * p0 * s1 + p1 * (2.0 * p0 * s2 + p1 * s3))
    x0, x1 = a0 + a1 * p0, a1 * p1
    z1, z2 = z1 - a1 * p0, -(a1 * p1)
    n2 = s0 + z1 * (2.0 * s1 + z1 * s2) + z2 * (2.0 * (s2 + z1 * s3) + z2 * s4)
    b1 = n2 / n1
    p0, p1, p2 = 1.0 + b1 * p0, z1 + b1 * p1, z2
    energy = p0 * p0 * s1 + p1 * (2.0 * p0 * s2 + p1 * s3) + p2 * (2.0 * (p0 * s3 + p1 * s4) + p2 * s5)
    a2 = n2 / energy
    return x0 + a2 * p0, x1 + a2 * p1, a2 * p2


def solved(recv_ref):
    total = tree([recv_ref[s] for s in range(SLABS)])
    return weights([jnp.broadcast_to(total[:1, 48 + n : 49 + n], (8, 128)) for n in range(6)])


def combine_kernel(recv_ref, ret_ref, out_ref):
    w0, w1, w2 = solved(recv_ref)
    for l in range(LAYERS):
        for n in range(4):
            out_ref[l, n] = w0 * ret_ref[l, n] + w1 * ret_ref[l, 4 + n] + w2 * ret_ref[l, 8 + n]


def finish_kernel(rows_ref, recv_ref, back_ref, adjoint_ref, owned_ref):
    lane = lanes()
    sub = sublanes()
    for j in range(LAYERS):
        for n in range(4):
            col = WIDTH * j + 128 * (n % 2)
            adjoint_ref[0, 8 * (n // 2) : 8 * (n // 2) + 8, col : col + 128] = back_ref[j, n]
    w0, w1, w2 = solved(recv_ref)
    for k in range(OWNED):
        row = rows_ref[k]
        tile = jnp.zeros((8, 128), F32)
        for i in range(PER_TILE):
            half = recv_ref[PER_TILE * row + i]
            whole = jnp.concatenate([half, half], axis=0)
            strip = jnp.where(sub < 4, whole, pltpu.roll(whole, 64, axis=1))
            value = w0 * strip + w1 * pltpu.roll(strip, 112, axis=1) + w2 * pltpu.roll(strip, 96, axis=1)
            if i:
                value = pltpu.roll(value, 16 * i, axis=1)
            tile = jnp.where((lane >= 16 * i) & (lane < 16 * i + 16), value, tile)
        owned_ref[k] = tile


VMEM = pl.BlockSpec(memory_space=pltpu.VMEM)
SMEM = pl.BlockSpec(memory_space=pltpu.SMEM)


def shape(*dims):
    return jax.ShapeDtypeStruct(dims, F32)


def call(kernel, ins, outs, scratch=(), interpret=False):
    single = len(outs) == 1
    return pl.pallas_call(
        kernel,
        out_shape=outs[0] if single else tuple(outs),
        in_specs=ins,
        out_specs=VMEM if single else tuple(VMEM for _ in outs),
        scratch_shapes=list(scratch),
        compiler_params=pltpu.CompilerParams(vmem_limit_bytes=VMEM_LIMIT),
        interpret=interpret,
    )


def pack(both, owner, interpret=False):
    outs = [shape(LAYERS, 9, 8, 128), jax.ShapeDtypeStruct(owner.shape, owner.dtype)]
    return call(pack_kernel, [VMEM] * 2, outs, interpret=interpret)(both, owner)


def halo(turn, recv, interpret=False):
    side = shape(2 * LAYERS + 1, 8, 128)
    return call(halo_kernel, [SMEM, VMEM], [side, side], interpret=interpret)(turn, recv)


def stage(recv, interpret=False):
    block = shape(LAYERS, ROWS, EXT_COLS)
    outs = [shape(LAYERS + 1, ROWS, EXT_COLS)] + [block] * 4
    return call(stage_kernel, [VMEM], outs, interpret=interpret)(recv)


def krylov(turn, first, second, staged, interpret=False):
    field = pltpu.VMEM((LAYERS + 1, EXT_ROWS, EXT_COLS), F32)
    face = pltpu.VMEM((LAYERS, EXT_ROWS, EXT_COLS), F32)
    rim = pltpu.VMEM((LAYERS + 1, EXT_ROWS - ROWS, EXT_COLS), F32)
    return call(
        krylov_kernel,
        [SMEM] + [VMEM] * 7,
        [shape(LAYERS, 8, 128), shape(LAYERS, 12, 8, 128)],
        [rim, field, field, field, face, rim, face, rim, pltpu.VMEM((128, 128), F32)],
        interpret=interpret,
    )(turn, first, second, *staged)


def route(owner, index, recv, interpret=False):
    return call(route_kernel, [SMEM, SMEM, VMEM], [shape(SLABS, 4, 128)], interpret=interpret)(owner, index, recv)


def combine(recv, ret, interpret=False):
    return call(combine_kernel, [VMEM] * 2, [shape(LAYERS, 4, 8, 128)], interpret=interpret)(recv, ret)


def finish(rows, recv, back, interpret=False):
    outs = [shape(1, ROWS, COLS), shape(OWNED, 8, 128)]
    return call(finish_kernel, [SMEM, VMEM, VMEM], outs, interpret=interpret)(rows, recv, back)


def owned_rows(tile_owner, index):
    held = jnp.any(tile_owner == index, axis=1)
    rank = jnp.cumsum(held.astype(jnp.int32)) - 1
    slot = jnp.arange(OWNED, dtype=jnp.int32)[:, None]
    row = jnp.arange(tile_owner.shape[0], dtype=jnp.int32)[None, :]
    return jnp.sum(jnp.where(held[None, :] & (rank[None, :] == slot), row, 0), axis=1)


def pairing(first):
    pairs = [(low, low + 1) for low in range(first, SLABS - 1, 2)]
    return pairs + [(high, low) for low, high in pairs]


def per_device(adjoint_source, conductivity, tile_owner):
    index = lax.axis_index("slab")
    place = index.reshape(1)
    turn = (index + 1).reshape(1)
    both = jnp.concatenate([conductivity, adjoint_source], axis=0)
    packed, table = pack(both, tile_owner)
    recv = lax.all_to_all(packed, "layer", 0, 0, tiled=True)
    first, second = halo(turn, recv)
    first, second, recv, table = lax.optimization_barrier((first, second, recv, table))
    staged = stage(recv)
    rows = owned_rows(table, index)
    first = lax.ppermute(first, "slab", pairing(1))
    second = lax.ppermute(second, "slab", pairing(0))
    first, second, rows = lax.optimization_barrier((first, second, rows))
    msg, ret = krylov(turn, first, second, staged)
    strips = lax.all_to_all(msg, "layer", 0, 0, tiled=True)
    outgoing = route(table, place, strips)
    received = lax.all_to_all(outgoing, "slab", 0, 0, tiled=True)
    back = lax.all_to_all(combine(received, ret), "layer", 0, 0, tiled=True)
    return finish(rows, received, back)


def solution(mesh):
    placed = (P("layer", "slab", None), P("layer", "slab", None), P())
    return jax.shard_map(
        per_device,
        mesh=mesh,
        in_specs=placed,
        out_specs=(P("layer", "slab", None), P("slab", "layer", None)),
        check_vma=False,
    )
```

```python
import jax
import jax.numpy as jnp
from jax import lax
from jax.experimental import pallas as pl
from jax.experimental.pallas import tpu as pltpu
from jax.sharding import PartitionSpec as P

F32 = jnp.float32
LAYERS = 16
ROWS = 16
COLS = 4096
WIDTH = COLS // LAYERS
SLABS = 64
TILE_COLS = 32
PER_TILE = 8
OWNED = 4
EXT_ROWS = 24
EXT_COLS = 384
SCALE = 2.0**-6
VMEM_LIMIT = 48 * 1024 * 1024


def lanes():
    return lax.broadcasted_iota(jnp.int32, (8, 128), 1)


def sublanes():
    return lax.broadcasted_iota(jnp.int32, (8, 128), 0)


def pack_kernel(turn_ref, both_ref, owner_ref, out_ref, table_ref):
    lane = lanes()
    zero = jnp.zeros((8, 128), F32)
    table_ref[...] = owner_ref[...]
    for j in range(LAYERS):
        edge = zero
        for q in range(2):
            for g in range(2):
                rows = slice(8 * g, 8 * g + 8)
                base = WIDTH * j
                for t in range(2):
                    out_ref[j, 4 * q + 2 * g + t] = both_ref[q, rows, base + 128 * t : base + 128 * t + 128]
                before = both_ref[q, rows, base - 128 : base] if j > 0 else zero
                after = both_ref[q, rows, base + 256 : base + 384] if j < LAYERS - 1 else zero
                both = jnp.where(lane < 4, after, jnp.where(lane >= 124, before, 0.0))
                edge = edge + pltpu.roll(both, 4 + 8 * (2 * g + q), axis=1)
        out_ref[j, 8] = edge


def halo_kernel(turn_ref, recv_ref, first_ref, second_ref):
    even = turn_ref[0] % 2 == 0

    def put(n, up, down):
        first_ref[n] = jnp.where(even, up, down)
        second_ref[n] = jnp.where(even, down, up)

    lane = lanes()
    sub = sublanes()
    up_edges = [jnp.zeros((8, 128), F32)] * 2
    down_edges = [jnp.zeros((8, 128), F32)] * 2
    for l in range(LAYERS):
        for t in range(2):
            up = jnp.where(sub >= 4, recv_ref[l, 2 + t], pltpu.roll(recv_ref[l, 6 + t], 4, axis=0))
            down = jnp.where(sub < 4, recv_ref[l, t], pltpu.roll(recv_ref[l, 4 + t], 4, axis=0))
            put(2 * l + t, up, down)
        edge = recv_ref[l, 8]
        half, place = l // 8, 16 * (l % 8)
        here = (lane >= place) & (lane < place + 16)
        up_edges[half] = jnp.where(here, pltpu.roll(edge, (place + 112) % 128, axis=1), up_edges[half])
        down_edges[half] = jnp.where(here, pltpu.roll(edge, place, axis=1), down_edges[half])
    up = jnp.where(sub >= 4, up_edges[0], pltpu.roll(up_edges[1], 4, axis=0))
    down = jnp.where(sub < 4, down_edges[0], pltpu.roll(down_edges[1], 4, axis=0))
    put(32, up, down)


def own(value):
    return value[:ROWS, :WIDTH]


def folded(value):
    return (value[:8, :128] + value[8:, :128]) + (value[:8, 128:] + value[8:, 128:])


def krylov_kernel(
    turn_ref, recv_ref, first_ref, second_ref, msg_ref, ret_ref, k_ref, v0_ref, v1_ref, v2_ref, inv_ref, cc_ref, cr_ref, cz_ref, square_ref
):
    lane = lanes()
    sub = sublanes()
    rim = (lane < 4) | (lane >= 124)
    blank = jnp.zeros((EXT_ROWS, EXT_COLS), F32)
    for ref in (k_ref, v0_ref, v1_ref, v2_ref):
        ref[LAYERS] = blank

    def spread(tile, place):
        return jnp.where(rim, pltpu.roll(tile, (252 - place) % 128, axis=1), 0.0)

    even = turn_ref[0] % 2 == 0
    upper = (sub < 4) == even

    def halves(n):
        one, two = first_ref[n], second_ref[n]
        return jnp.where(upper, one, two), pltpu.roll(jnp.where(upper, two, one), 4, axis=0)

    halo_edges = halves(32)
    for l in range(LAYERS):
        edge = recv_ref[l, 8]
        for q, ref in enumerate((k_ref, v0_ref)):
            for g in range(2):
                for t in range(2):
                    ref[l, 8 * g : 8 * g + 8, 128 * t : 128 * t + 128] = recv_ref[l, 4 * q + 2 * g + t]
                ref[l, 8 * g : 8 * g + 8, 256:384] = spread(edge, 8 * (2 * g + q))
            ref[l, 16:24, 256:384] = spread(halo_edges[l // 8], 16 * (l % 8) + 8 * q)
        for t in range(2):
            cols = slice(128 * t, 128 * t + 128)
            k_ref[l, 16:24, cols], v0_ref[l, 16:24, cols] = halves(2 * l + t)

    def setup(l, carry):
        cz_before, s0, m0 = carry
        k = k_ref[l]
        cc = k + pltpu.roll(k, EXT_COLS - 1, axis=1)
        cr = k + pltpu.roll(k, EXT_ROWS - 1, axis=0)
        cz = k + k_ref[l + 1]
        diag = (cc + pltpu.roll(cc, 1, axis=1)) + (cr + pltpu.roll(cr, 1, axis=0)) + (cz + cz_before)
        inv = jnp.where(k > 0.0, 1.0 / diag, 0.0)
        twice = v0_ref[l] * 2.0
        v0 = twice * inv
        cc_ref[l] = cc
        cr_ref[l] = cr
        cz_ref[l] = cz
        inv_ref[l] = inv
        v0_ref[l] = v0
        mine = own(v0)
        for g in range(2):
            for t in range(2):
                ret_ref[l, 2 * g + t] = mine[8 * g : 8 * g + 8, 128 * t : 128 * t + 128]
        return cz, s0 + folded(mine * (own(twice) * SCALE)), m0 + mine

    none = jnp.zeros((8, 128), F32)
    no_map = jnp.zeros((ROWS, WIDTH), F32)
    _, s0, m0 = lax.fori_loop(0, LAYERS, setup, (k_ref[0], none, no_map), unroll=8)

    def image(l, v_ref, fz_before):
        v = v_ref[l]
        fc = cc_ref[l] * (v - pltpu.roll(v, EXT_COLS - 1, axis=1))
        fr = cr_ref[l] * (v - pltpu.roll(v, EXT_ROWS - 1, axis=0))
        fz = cz_ref[l] * (v - v_ref[l + 1])
        result = (fc - pltpu.roll(fc, 1, axis=1)) + (fr - pltpu.roll(fr, 1, axis=0)) + (fz - fz_before)
        return v, result, fz

    def step(v_ref, out_ref, slot):
        def body(l, carry):
            fz_before, odd, even, total = carry
            v, result, fz = image(l, v_ref, fz_before)
            after = inv_ref[l] * result
            out_ref[l] = after
            mine = own(after)
            for g in range(2):
                for t in range(2):
                    ret_ref[l, 4 * slot + 2 * g + t] = mine[8 * g : 8 * g + 8, 128 * t : 128 * t + 128]
            got = own(result) * SCALE
            return fz, odd + folded(own(v) * got), even + folded(mine * got), total + mine

        start = (-(k_ref[0] * v_ref[0]), none, none, no_map)
        return lax.fori_loop(0, LAYERS, body, start, unroll=8)[1:]

    s1, s2, m1 = step(v0_ref, v1_ref, 1)
    s3, s4, m2 = step(v1_ref, v2_ref, 2)

    def last(l, carry):
        fz_before, odd = carry
        v, result, fz = image(l, v2_ref, fz_before)
        return fz, odd + folded(own(v) * (own(result) * SCALE))

    _, s5 = lax.fori_loop(0, LAYERS, last, (-(k_ref[0] * v2_ref[0]), none), unroll=16)

    sums = none
    for n, part in enumerate((s0, s1, s2, s3, s4, s5)):
        sums = jnp.where(sub == n, jnp.sum(part), sums)
    first = lax.broadcasted_iota(jnp.int32, (ROWS, 128), 1) % 8 < 4
    for f, total in enumerate((m0, m1, m2)):
        left, right = total[:, :128], total[:, 128:]
        square_ref[16 * f : 16 * f + 16, :] = jnp.where(first, left, pltpu.roll(right, 4, axis=1))
        square_ref[64 + 16 * f : 80 + 16 * f, :] = jnp.where(first, pltpu.roll(left, 124, axis=1), right)
    square_ref[48:56, :] = sums
    square_ref[56:64, :] = none
    square_ref[112:120, :] = none
    square_ref[120:128, :] = none
    turned = square_ref[...].T
    for j in range(LAYERS):
        msg_ref[j] = turned[8 * j : 8 * j + 8, :]


def tree(values):
    while len(values) > 1:
        values = [a + b for a, b in zip(values[::2], values[1::2])]
    return values[0]


def route_kernel(owner_ref, index_ref, recv_ref, msg_ref):
    lane = lax.broadcasted_iota(jnp.int32, (4, 128), 1)
    shared = (lane >= 48) & (lane < 64)
    total = tree([recv_ref[j] for j in range(LAYERS)])
    common = total[:4]
    for o in range(SLABS):
        msg_ref[o] = common
    row = index_ref[0] // PER_TILE
    for c in range(TILE_COLS):
        half = 4 * (c % 2)
        strip = recv_ref[c // 2, half : half + 4]
        msg_ref[owner_ref[row, c]] = jnp.where(shared, common, strip)


def weights(s):
    level = jnp.where(s[0] > 2.0**60, 2.0**-60, jnp.where(s[0] < 2.0**-60, 2.0**60, 1.0))
    s0, s1, s2, s3, s4, s5 = [value * level for value in s]
    a0 = s0 / s1
    z1 = -a0
    n1 = s0 + z1 * (2.0 * s1 + z1 * s2)
    b0 = n1 / s0
    p0, p1 = 1.0 + b0, z1
    a1 = n1 / (p0 * p0 * s1 + p1 * (2.0 * p0 * s2 + p1 * s3))
    x0, x1 = a0 + a1 * p0, a1 * p1
    z1, z2 = z1 - a1 * p0, -(a1 * p1)
    n2 = s0 + z1 * (2.0 * s1 + z1 * s2) + z2 * (2.0 * (s2 + z1 * s3) + z2 * s4)
    b1 = n2 / n1
    p0, p1, p2 = 1.0 + b1 * p0, z1 + b1 * p1, z2
    energy = p0 * p0 * s1 + p1 * (2.0 * p0 * s2 + p1 * s3) + p2 * (2.0 * (p0 * s3 + p1 * s4) + p2 * s5)
    a2 = n2 / energy
    return x0 + a2 * p0, x1 + a2 * p1, a2 * p2


def solved(recv_ref):
    total = tree([recv_ref[s] for s in range(SLABS)])
    return weights([jnp.broadcast_to(total[:1, 48 + n : 49 + n], (8, 128)) for n in range(6)])


def combine_kernel(recv_ref, ret_ref, out_ref):
    w0, w1, w2 = solved(recv_ref)
    for l in range(LAYERS):
        for n in range(4):
            out_ref[l, n] = w0 * ret_ref[l, n] + w1 * ret_ref[l, 4 + n] + w2 * ret_ref[l, 8 + n]


def finish_kernel(rows_ref, recv_ref, back_ref, adjoint_ref, owned_ref):
    lane = lanes()
    sub = sublanes()
    for j in range(LAYERS):
        for n in range(4):
            col = WIDTH * j + 128 * (n % 2)
            adjoint_ref[0, 8 * (n // 2) : 8 * (n // 2) + 8, col : col + 128] = back_ref[j, n]
    w0, w1, w2 = solved(recv_ref)
    for k in range(OWNED):
        row = rows_ref[k]
        tile = jnp.zeros((8, 128), F32)
        for i in range(PER_TILE):
            half = recv_ref[PER_TILE * row + i]
            whole = jnp.concatenate([half, half], axis=0)
            strip = jnp.where(sub < 4, whole, pltpu.roll(whole, 64, axis=1))
            value = w0 * strip + w1 * pltpu.roll(strip, 112, axis=1) + w2 * pltpu.roll(strip, 96, axis=1)
            if i:
                value = pltpu.roll(value, 16 * i, axis=1)
            tile = jnp.where((lane >= 16 * i) & (lane < 16 * i + 16), value, tile)
        owned_ref[k] = tile


VMEM = pl.BlockSpec(memory_space=pltpu.VMEM)
SMEM = pl.BlockSpec(memory_space=pltpu.SMEM)


def shape(*dims):
    return jax.ShapeDtypeStruct(dims, F32)


def call(kernel, ins, outs, scratch=(), interpret=False):
    single = len(outs) == 1
    return pl.pallas_call(
        kernel,
        out_shape=outs[0] if single else tuple(outs),
        in_specs=ins,
        out_specs=VMEM if single else tuple(VMEM for _ in outs),
        scratch_shapes=list(scratch),
        compiler_params=pltpu.CompilerParams(vmem_limit_bytes=VMEM_LIMIT),
        interpret=interpret,
    )


def pack(turn, both, owner, interpret=False):
    outs = [shape(LAYERS, 9, 8, 128), jax.ShapeDtypeStruct(owner.shape, owner.dtype)]
    return call(pack_kernel, [SMEM] + [VMEM] * 2, outs, interpret=interpret)(turn, both, owner)


def halo(turn, recv, interpret=False):
    side = shape(2 * LAYERS + 1, 8, 128)
    return call(halo_kernel, [SMEM, VMEM], [side, side], interpret=interpret)(turn, recv)


def krylov(turn, recv, first, second, interpret=False):
    field = pltpu.VMEM((LAYERS + 1, EXT_ROWS, EXT_COLS), F32)
    face = pltpu.VMEM((LAYERS, EXT_ROWS, EXT_COLS), F32)
    return call(
        krylov_kernel,
        [SMEM] + [VMEM] * 3,
        [shape(LAYERS, 8, 128), shape(LAYERS, 12, 8, 128)],
        [field] * 4 + [face] * 4 + [pltpu.VMEM((128, 128), F32)],
        interpret=interpret,
    )(turn, recv, first, second)


def route(owner, index, recv, interpret=False):
    return call(route_kernel, [SMEM, SMEM, VMEM], [shape(SLABS, 4, 128)], interpret=interpret)(owner, index, recv)


def combine(recv, ret, interpret=False):
    return call(combine_kernel, [VMEM] * 2, [shape(LAYERS, 4, 8, 128)], interpret=interpret)(recv, ret)


def finish(rows, recv, back, interpret=False):
    outs = [shape(1, ROWS, COLS), shape(OWNED, 8, 128)]
    return call(finish_kernel, [SMEM, VMEM, VMEM], outs, interpret=interpret)(rows, recv, back)


def owned_rows(tile_owner, index):
    held = jnp.any(tile_owner == index, axis=1)
    rank = jnp.cumsum(held.astype(jnp.int32)) - 1
    slot = jnp.arange(OWNED, dtype=jnp.int32)[:, None]
    row = jnp.arange(tile_owner.shape[0], dtype=jnp.int32)[None, :]
    return jnp.sum(jnp.where(held[None, :] & (rank[None, :] == slot), row, 0), axis=1)


def pairing(first):
    pairs = [(low, low + 1) for low in range(first, SLABS - 1, 2)]
    return pairs + [(high, low) for low, high in pairs]


def per_device(adjoint_source, conductivity, tile_owner):
    index = lax.axis_index("slab")
    place = index.reshape(1)
    turn = (index + 1).reshape(1)
    both = jnp.concatenate([conductivity, adjoint_source], axis=0)
    packed, table = pack(turn, both, tile_owner)
    recv = lax.all_to_all(packed, "layer", 0, 0, tiled=True)
    first, second = halo(turn, recv)
    first, table = lax.optimization_barrier((first, table))
    rows = owned_rows(table, index)
    first = lax.ppermute(first, "slab", pairing(1))
    second = lax.ppermute(second, "slab", pairing(0))
    first, second, rows = lax.optimization_barrier((first, second, rows))
    msg, ret = krylov(turn, recv, first, second)
    strips = lax.all_to_all(msg, "layer", 0, 0, tiled=True)
    outgoing = route(table, place, strips)
    received = lax.all_to_all(outgoing, "slab", 0, 0, tiled=True)
    back = lax.all_to_all(combine(received, ret), "layer", 0, 0, tiled=True)
    return finish(rows, received, back)


def solution(mesh):
    placed = (P("layer", "slab", None), P("layer", "slab", None), P())
    return jax.shard_map(
        per_device,
        mesh=mesh,
        in_specs=placed,
        out_specs=(P("layer", "slab", None), P("slab", "layer", None)),
        check_vma=False,
    )
```

```python
import jax
import jax.numpy as jnp
from jax import lax
from jax.experimental import pallas as pl
from jax.experimental.pallas import tpu as pltpu
from jax.sharding import PartitionSpec as P

F32 = jnp.float32
LAYERS = 16
ROWS = 16
COLS = 4096
WIDTH = COLS // LAYERS
SLABS = 64
TILE_COLS = 32
PER_TILE = 8
OWNED = 4
EXT_ROWS = 24
EXT_COLS = 384
SCALE = 2.0**-6
VMEM_LIMIT = 48 * 1024 * 1024


def lanes():
    return lax.broadcasted_iota(jnp.int32, (8, 128), 1)


def sublanes():
    return lax.broadcasted_iota(jnp.int32, (8, 128), 0)


def pack_kernel(turn_ref, both_ref, owner_ref, out_ref, table_ref):
    lane = lanes()
    zero = jnp.zeros((8, 128), F32)
    table_ref[...] = owner_ref[...]
    for j in range(LAYERS):
        edge = zero
        for q in range(2):
            for g in range(2):
                rows = slice(8 * g, 8 * g + 8)
                base = WIDTH * j
                for t in range(2):
                    out_ref[j, 4 * q + 2 * g + t] = both_ref[q, rows, base + 128 * t : base + 128 * t + 128]
                before = both_ref[q, rows, base - 128 : base] if j > 0 else zero
                after = both_ref[q, rows, base + 256 : base + 384] if j < LAYERS - 1 else zero
                both = jnp.where(lane < 4, after, jnp.where(lane >= 124, before, 0.0))
                edge = edge + pltpu.roll(both, 4 + 8 * (2 * g + q), axis=1)
        out_ref[j, 8] = edge


def halo_kernel(turn_ref, recv_ref, first_ref, second_ref):
    even = turn_ref[0] % 2 == 0

    def put(n, up, down):
        first_ref[n] = jnp.where(even, up, down)
        second_ref[n] = jnp.where(even, down, up)

    lane = lanes()
    sub = sublanes()
    up_edges = [jnp.zeros((8, 128), F32)] * 2
    down_edges = [jnp.zeros((8, 128), F32)] * 2
    for l in range(LAYERS):
        for t in range(2):
            up = jnp.where(sub >= 4, recv_ref[l, 2 + t], pltpu.roll(recv_ref[l, 6 + t], 4, axis=0))
            down = jnp.where(sub < 4, recv_ref[l, t], pltpu.roll(recv_ref[l, 4 + t], 4, axis=0))
            put(2 * l + t, up, down)
        edge = recv_ref[l, 8]
        half, place = l // 8, 16 * (l % 8)
        here = (lane >= place) & (lane < place + 16)
        up_edges[half] = jnp.where(here, pltpu.roll(edge, (place + 112) % 128, axis=1), up_edges[half])
        down_edges[half] = jnp.where(here, pltpu.roll(edge, place, axis=1), down_edges[half])
    up = jnp.where(sub >= 4, up_edges[0], pltpu.roll(up_edges[1], 4, axis=0))
    down = jnp.where(sub < 4, down_edges[0], pltpu.roll(down_edges[1], 4, axis=0))
    put(32, up, down)


def own(value):
    return value[:ROWS, :WIDTH]


def folded(value):
    return (value[:8, :128] + value[8:, :128]) + (value[:8, 128:] + value[8:, 128:])


def spread(tile, place):
    lane = lanes()
    return jnp.where((lane < 4) | (lane >= 124), pltpu.roll(tile, (252 - place) % 128, axis=1), 0.0)


def stage_kernel(recv_ref, k_ref, s_ref, cc_ref, cz_ref, diag_ref):
    k_ref[LAYERS] = jnp.zeros((ROWS, EXT_COLS), F32)
    for l in range(LAYERS):
        edge = recv_ref[l, 8]
        for q, ref in enumerate((k_ref, s_ref)):
            for g in range(2):
                rows = slice(8 * g, 8 * g + 8)
                for t in range(2):
                    ref[l, rows, 128 * t : 128 * t + 128] = recv_ref[l, 4 * q + 2 * g + t]
                ref[l, rows, 256:384] = spread(edge, 8 * (2 * g + q))

    def body(l, cz_before):
        k = k_ref[l]
        cc = k + pltpu.roll(k, EXT_COLS - 1, axis=1)
        cz = k + k_ref[l + 1]
        cc_ref[l] = cc
        cz_ref[l] = cz
        diag_ref[l] = (cc + pltpu.roll(cc, 1, axis=1)) + (cz + cz_before)
        return cz

    lax.fori_loop(0, LAYERS, body, k_ref[0], unroll=8)


def krylov_kernel(
    turn_ref, first_ref, second_ref, own_k_ref, own_s_ref, own_cc_ref, own_cz_ref, own_diag_ref, msg_ref, ret_ref,
    k_ref, v0_ref, v1_ref, v2_ref, inv_ref, cc_ref, cr_ref, cz_ref, square_ref
):
    sub = sublanes()
    blank = jnp.zeros((EXT_ROWS, EXT_COLS), F32)
    k_ref[LAYERS] = blank[ROWS:]
    for ref in (v0_ref, v1_ref, v2_ref):
        ref[LAYERS] = blank

    even = turn_ref[0] % 2 == 0
    upper = (sub < 4) == even

    def halves(n):
        one, two = first_ref[n], second_ref[n]
        return jnp.where(upper, one, two), pltpu.roll(jnp.where(upper, two, one), 4, axis=0)

    halo_edges = halves(32)
    for l in range(LAYERS):
        place = 16 * (l % 8)
        k_ref[l, :, 256:384] = spread(halo_edges[l // 8], place)
        v0_ref[l, 16:24, 256:384] = spread(halo_edges[l // 8], place + 8)
        for t in range(2):
            cols = slice(128 * t, 128 * t + 128)
            k_ref[l, :, cols], v0_ref[l, 16:24, cols] = halves(2 * l + t)

    def joined(own_ref, rim_ref, l):
        return jnp.concatenate([own_ref[l], rim_ref[l]], axis=0)

    def setup(l, carry):
        cz_before, s0, m0 = carry
        rim = k_ref[l]
        cc = rim + pltpu.roll(rim, EXT_COLS - 1, axis=1)
        cz = rim + k_ref[l + 1]
        cc_ref[l] = cc
        cz_ref[l] = cz
        diag = (cc + pltpu.roll(cc, 1, axis=1)) + (cz + cz_before)
        k = joined(own_k_ref, k_ref, l)
        cr = k + pltpu.roll(k, EXT_ROWS - 1, axis=0)
        cr_ref[l] = cr
        diag = jnp.concatenate([own_diag_ref[l], diag], axis=0) + (cr + pltpu.roll(cr, 1, axis=0))
        inv = jnp.where(k > 0.0, 1.0 / diag, 0.0)
        twice = jnp.concatenate([own_s_ref[l], v0_ref[l, 16:24, :]], axis=0) * 2.0
        v0 = twice * inv
        inv_ref[l] = inv
        v0_ref[l] = v0
        mine = own(v0)
        for g in range(2):
            for t in range(2):
                ret_ref[l, 2 * g + t] = mine[8 * g : 8 * g + 8, 128 * t : 128 * t + 128]
        return cz, s0 + folded(mine * (own(twice) * SCALE)), m0 + mine

    none = jnp.zeros((8, 128), F32)
    no_map = jnp.zeros((ROWS, WIDTH), F32)
    _, s0, m0 = lax.fori_loop(0, LAYERS, setup, (k_ref[0], none, no_map), unroll=8)

    def image(l, v_ref, fz_before):
        v = v_ref[l]
        fc = joined(own_cc_ref, cc_ref, l) * (v - pltpu.roll(v, EXT_COLS - 1, axis=1))
        fr = cr_ref[l] * (v - pltpu.roll(v, EXT_ROWS - 1, axis=0))
        fz = joined(own_cz_ref, cz_ref, l) * (v - v_ref[l + 1])
        result = (fc - pltpu.roll(fc, 1, axis=1)) + (fr - pltpu.roll(fr, 1, axis=0)) + (fz - fz_before)
        return v, result, fz

    def step(v_ref, out_ref, slot):
        def body(l, carry):
            fz_before, odd, even, total = carry
            v, result, fz = image(l, v_ref, fz_before)
            after = inv_ref[l] * result
            out_ref[l] = after
            mine = own(after)
            for g in range(2):
                for t in range(2):
                    ret_ref[l, 4 * slot + 2 * g + t] = mine[8 * g : 8 * g + 8, 128 * t : 128 * t + 128]
            got = own(result) * SCALE
            return fz, odd + folded(own(v) * got), even + folded(mine * got), total + mine

        start = (-(joined(own_k_ref, k_ref, 0) * v_ref[0]), none, none, no_map)
        return lax.fori_loop(0, LAYERS, body, start, unroll=8)[1:]

    s1, s2, m1 = step(v0_ref, v1_ref, 1)
    s3, s4, m2 = step(v1_ref, v2_ref, 2)

    def last(l, carry):
        fz_before, odd = carry
        v, result, fz = image(l, v2_ref, fz_before)
        return fz, odd + folded(own(v) * (own(result) * SCALE))

    _, s5 = lax.fori_loop(0, LAYERS, last, (-(joined(own_k_ref, k_ref, 0) * v2_ref[0]), none), unroll=16)

    sums = none
    for n, part in enumerate((s0, s1, s2, s3, s4, s5)):
        sums = jnp.where(sub == n, jnp.sum(part, axis=0, keepdims=True), sums)
    sums = jnp.broadcast_to(jnp.sum(sums, axis=1, keepdims=True), (8, 128))
    first = lax.broadcasted_iota(jnp.int32, (ROWS, 128), 1) % 8 < 4
    for f, total in enumerate((m0, m1, m2)):
        left, right = total[:, :128], total[:, 128:]
        square_ref[16 * f : 16 * f + 16, :] = jnp.where(first, left, pltpu.roll(right, 4, axis=1))
        square_ref[64 + 16 * f : 80 + 16 * f, :] = jnp.where(first, pltpu.roll(left, 124, axis=1), right)
    square_ref[48:56, :] = sums
    square_ref[56:64, :] = none
    square_ref[112:120, :] = none
    square_ref[120:128, :] = none
    turned = square_ref[...].T
    for j in range(LAYERS):
        msg_ref[j] = turned[8 * j : 8 * j + 8, :]


def tree(values):
    while len(values) > 1:
        values = [a + b for a, b in zip(values[::2], values[1::2])]
    return values[0]


def route_kernel(owner_ref, index_ref, recv_ref, msg_ref):
    lane = lax.broadcasted_iota(jnp.int32, (4, 128), 1)
    shared = (lane >= 48) & (lane < 64)
    total = tree([recv_ref[j] for j in range(LAYERS)])
    common = total[:4]
    for o in range(SLABS):
        msg_ref[o] = common
    row = index_ref[0] // PER_TILE
    for c in range(TILE_COLS):
        half = 4 * (c % 2)
        strip = recv_ref[c // 2, half : half + 4]
        msg_ref[owner_ref[row, c]] = jnp.where(shared, common, strip)


def weights(s):
    level = jnp.where(s[0] > 2.0**60, 2.0**-60, jnp.where(s[0] < 2.0**-60, 2.0**60, 1.0))
    s0, s1, s2, s3, s4, s5 = [value * level for value in s]
    a0 = s0 / s1
    z1 = -a0
    n1 = s0 + z1 * (2.0 * s1 + z1 * s2)
    b0 = n1 / s0
    p0, p1 = 1.0 + b0, z1
    a1 = n1 / (p0 * p0 * s1 + p1 * (2.0 * p0 * s2 + p1 * s3))
    x0, x1 = a0 + a1 * p0, a1 * p1
    z1, z2 = z1 - a1 * p0, -(a1 * p1)
    n2 = s0 + z1 * (2.0 * s1 + z1 * s2) + z2 * (2.0 * (s2 + z1 * s3) + z2 * s4)
    b1 = n2 / n1
    p0, p1, p2 = 1.0 + b1 * p0, z1 + b1 * p1, z2
    energy = p0 * p0 * s1 + p1 * (2.0 * p0 * s2 + p1 * s3) + p2 * (2.0 * (p0 * s3 + p1 * s4) + p2 * s5)
    a2 = n2 / energy
    return x0 + a2 * p0, x1 + a2 * p1, a2 * p2


def solved(recv_ref):
    total = tree([recv_ref[s] for s in range(SLABS)])
    return weights([jnp.broadcast_to(total[:1, 48 + n : 49 + n], (8, 128)) for n in range(6)])


def combine_kernel(recv_ref, ret_ref, out_ref):
    w0, w1, w2 = solved(recv_ref)
    for l in range(LAYERS):
        for n in range(4):
            out_ref[l, n] = w0 * ret_ref[l, n] + w1 * ret_ref[l, 4 + n] + w2 * ret_ref[l, 8 + n]


def finish_kernel(rows_ref, recv_ref, back_ref, adjoint_ref, owned_ref):
    lane = lanes()
    sub = sublanes()
    for j in range(LAYERS):
        for n in range(4):
            col = WIDTH * j + 128 * (n % 2)
            adjoint_ref[0, 8 * (n // 2) : 8 * (n // 2) + 8, col : col + 128] = back_ref[j, n]
    w0, w1, w2 = solved(recv_ref)
    for k in range(OWNED):
        row = rows_ref[k]
        tile = jnp.zeros((8, 128), F32)
        for i in range(PER_TILE):
            half = recv_ref[PER_TILE * row + i]
            whole = jnp.concatenate([half, half], axis=0)
            strip = jnp.where(sub < 4, whole, pltpu.roll(whole, 64, axis=1))
            value = w0 * strip + w1 * pltpu.roll(strip, 112, axis=1) + w2 * pltpu.roll(strip, 96, axis=1)
            if i:
                value = pltpu.roll(value, 16 * i, axis=1)
            tile = jnp.where((lane >= 16 * i) & (lane < 16 * i + 16), value, tile)
        owned_ref[k] = tile


VMEM = pl.BlockSpec(memory_space=pltpu.VMEM)
SMEM = pl.BlockSpec(memory_space=pltpu.SMEM)


def shape(*dims):
    return jax.ShapeDtypeStruct(dims, F32)


def call(kernel, ins, outs, scratch=(), interpret=False):
    single = len(outs) == 1
    return pl.pallas_call(
        kernel,
        out_shape=outs[0] if single else tuple(outs),
        in_specs=ins,
        out_specs=VMEM if single else tuple(VMEM for _ in outs),
        scratch_shapes=list(scratch),
        compiler_params=pltpu.CompilerParams(vmem_limit_bytes=VMEM_LIMIT),
        interpret=interpret,
    )


def pack(turn, both, owner, interpret=False):
    outs = [shape(LAYERS, 9, 8, 128), jax.ShapeDtypeStruct(owner.shape, owner.dtype)]
    return call(pack_kernel, [SMEM] + [VMEM] * 2, outs, interpret=interpret)(turn, both, owner)


def halo(turn, recv, interpret=False):
    side = shape(2 * LAYERS + 1, 8, 128)
    return call(halo_kernel, [SMEM, VMEM], [side, side], interpret=interpret)(turn, recv)


def stage(recv, interpret=False):
    block = shape(LAYERS, ROWS, EXT_COLS)
    outs = [shape(LAYERS + 1, ROWS, EXT_COLS)] + [block] * 4
    return call(stage_kernel, [VMEM], outs, interpret=interpret)(recv)


def krylov(turn, first, second, staged, interpret=False):
    field = pltpu.VMEM((LAYERS + 1, EXT_ROWS, EXT_COLS), F32)
    face = pltpu.VMEM((LAYERS, EXT_ROWS, EXT_COLS), F32)
    rim = pltpu.VMEM((LAYERS + 1, EXT_ROWS - ROWS, EXT_COLS), F32)
    return call(
        krylov_kernel,
        [SMEM] + [VMEM] * 7,
        [shape(LAYERS, 8, 128), shape(LAYERS, 12, 8, 128)],
        [rim, field, field, field, face, rim, face, rim, pltpu.VMEM((128, 128), F32)],
        interpret=interpret,
    )(turn, first, second, *staged)


def route(owner, index, recv, interpret=False):
    return call(route_kernel, [SMEM, SMEM, VMEM], [shape(SLABS, 4, 128)], interpret=interpret)(owner, index, recv)


def combine(recv, ret, interpret=False):
    return call(combine_kernel, [VMEM] * 2, [shape(LAYERS, 4, 8, 128)], interpret=interpret)(recv, ret)


def finish(rows, recv, back, interpret=False):
    outs = [shape(1, ROWS, COLS), shape(OWNED, 8, 128)]
    return call(finish_kernel, [SMEM, VMEM, VMEM], outs, interpret=interpret)(rows, recv, back)


def owned_rows(tile_owner, index):
    held = jnp.any(tile_owner == index, axis=1)
    rank = jnp.cumsum(held.astype(jnp.int32)) - 1
    slot = jnp.arange(OWNED, dtype=jnp.int32)[:, None]
    row = jnp.arange(tile_owner.shape[0], dtype=jnp.int32)[None, :]
    return jnp.sum(jnp.where(held[None, :] & (rank[None, :] == slot), row, 0), axis=1)


def pairing(first):
    pairs = [(low, low + 1) for low in range(first, SLABS - 1, 2)]
    return pairs + [(high, low) for low, high in pairs]


def per_device(adjoint_source, conductivity, tile_owner):
    index = lax.axis_index("slab")
    place = index.reshape(1)
    turn = (index + 1).reshape(1)
    both = jnp.concatenate([conductivity, adjoint_source], axis=0)
    packed, table = pack(turn, both, tile_owner)
    recv = lax.all_to_all(packed, "layer", 0, 0, tiled=True)
    first, second = halo(turn, recv)
    first, second, recv, table = lax.optimization_barrier((first, second, recv, table))
    staged = stage(recv)
    rows = owned_rows(table, index)
    first = lax.ppermute(first, "slab", pairing(1))
    second = lax.ppermute(second, "slab", pairing(0))
    first, second, rows = lax.optimization_barrier((first, second, rows))
    msg, ret = krylov(turn, first, second, staged)
    strips = lax.all_to_all(msg, "layer", 0, 0, tiled=True)
    outgoing = route(table, place, strips)
    received = lax.all_to_all(outgoing, "slab", 0, 0, tiled=True)
    back = lax.all_to_all(combine(received, ret), "layer", 0, 0, tiled=True)
    return finish(rows, received, back)


def solution(mesh):
    placed = (P("layer", "slab", None), P("layer", "slab", None), P())
    return jax.shard_map(
        per_device,
        mesh=mesh,
        in_specs=placed,
        out_specs=(P("layer", "slab", None), P("slab", "layer", None)),
        check_vma=False,
    )
```

```python
import jax
import jax.numpy as jnp
from jax import lax
from jax.experimental import pallas as pl
from jax.experimental.pallas import tpu as pltpu
from jax.sharding import PartitionSpec as P

F32 = jnp.float32
LAYERS = 16
ROWS = 16
COLS = 4096
WIDTH = COLS // LAYERS
SLABS = 64
TILE_COLS = 32
PER_TILE = 8
OWNED = 4
EXT_ROWS = 24
EXT_COLS = 384
SCALE = 2.0**-6
VMEM_LIMIT = 48 * 1024 * 1024


def lanes():
    return lax.broadcasted_iota(jnp.int32, (8, 128), 1)


def sublanes():
    return lax.broadcasted_iota(jnp.int32, (8, 128), 0)


def pack_kernel(turn_ref, both_ref, owner_ref, out_ref, table_ref):
    lane = lanes()
    zero = jnp.zeros((8, 128), F32)
    table_ref[...] = owner_ref[...]
    for j in range(LAYERS):
        edge = zero
        for q in range(2):
            for g in range(2):
                rows = slice(8 * g, 8 * g + 8)
                base = WIDTH * j
                for t in range(2):
                    out_ref[j, 4 * q + 2 * g + t] = both_ref[q, rows, base + 128 * t : base + 128 * t + 128]
                before = both_ref[q, rows, base - 128 : base] if j > 0 else zero
                after = both_ref[q, rows, base + 256 : base + 384] if j < LAYERS - 1 else zero
                both = jnp.where(lane < 4, after, jnp.where(lane >= 124, before, 0.0))
                edge = edge + pltpu.roll(both, 4 + 8 * (2 * g + q), axis=1)
        out_ref[j, 8] = edge


def halo_kernel(turn_ref, recv_ref, first_ref, second_ref):
    even = turn_ref[0] % 2 == 0

    def put(n, up, down):
        first_ref[n] = jnp.where(even, up, down)
        second_ref[n] = jnp.where(even, down, up)

    lane = lanes()
    sub = sublanes()
    up_edges = [jnp.zeros((8, 128), F32)] * 2
    down_edges = [jnp.zeros((8, 128), F32)] * 2
    for l in range(LAYERS):
        for t in range(2):
            up = jnp.where(sub >= 4, recv_ref[l, 2 + t], pltpu.roll(recv_ref[l, 6 + t], 4, axis=0))
            down = jnp.where(sub < 4, recv_ref[l, t], pltpu.roll(recv_ref[l, 4 + t], 4, axis=0))
            put(2 * l + t, up, down)
        edge = recv_ref[l, 8]
        half, place = l // 8, 16 * (l % 8)
        here = (lane >= place) & (lane < place + 16)
        up_edges[half] = jnp.where(here, pltpu.roll(edge, (place + 112) % 128, axis=1), up_edges[half])
        down_edges[half] = jnp.where(here, pltpu.roll(edge, place, axis=1), down_edges[half])
    up = jnp.where(sub >= 4, up_edges[0], pltpu.roll(up_edges[1], 4, axis=0))
    down = jnp.where(sub < 4, down_edges[0], pltpu.roll(down_edges[1], 4, axis=0))
    put(32, up, down)


def own(value):
    return value[:ROWS, :WIDTH]


def folded(value):
    return (value[:8, :128] + value[8:, :128]) + (value[:8, 128:] + value[8:, 128:])


def krylov_kernel(
    turn_ref, recv_ref, first_ref, second_ref, msg_ref, ret_ref, k_ref, v0_ref, v1_ref, v2_ref, inv_ref, cc_ref, cr_ref, cz_ref, square_ref
):
    lane = lanes()
    sub = sublanes()
    rim = (lane < 4) | (lane >= 124)
    blank = jnp.zeros((EXT_ROWS, EXT_COLS), F32)
    for ref in (k_ref, v0_ref, v1_ref, v2_ref):
        ref[LAYERS] = blank

    def spread(tile, place):
        return jnp.where(rim, pltpu.roll(tile, (252 - place) % 128, axis=1), 0.0)

    even = turn_ref[0] % 2 == 0
    upper = (sub < 4) == even

    def halves(n):
        one, two = first_ref[n], second_ref[n]
        return jnp.where(upper, one, two), pltpu.roll(jnp.where(upper, two, one), 4, axis=0)

    halo_edges = halves(32)
    for l in range(LAYERS):
        edge = recv_ref[l, 8]
        for q, ref in enumerate((k_ref, v0_ref)):
            for g in range(2):
                for t in range(2):
                    ref[l, 8 * g : 8 * g + 8, 128 * t : 128 * t + 128] = recv_ref[l, 4 * q + 2 * g + t]
                ref[l, 8 * g : 8 * g + 8, 256:384] = spread(edge, 8 * (2 * g + q))
            ref[l, 16:24, 256:384] = spread(halo_edges[l // 8], 16 * (l % 8) + 8 * q)
        for t in range(2):
            cols = slice(128 * t, 128 * t + 128)
            k_ref[l, 16:24, cols], v0_ref[l, 16:24, cols] = halves(2 * l + t)

    def setup(l, carry):
        cz_before, s0, m0 = carry
        k = k_ref[l]
        cc = k + pltpu.roll(k, EXT_COLS - 1, axis=1)
        cr = k + pltpu.roll(k, EXT_ROWS - 1, axis=0)
        cz = k + k_ref[l + 1]
        diag = (cc + pltpu.roll(cc, 1, axis=1)) + (cr + pltpu.roll(cr, 1, axis=0)) + (cz + cz_before)
        inv = jnp.where(k > 0.0, 1.0 / diag, 0.0)
        twice = v0_ref[l] * 2.0
        v0 = twice * inv
        cc_ref[l] = cc
        cr_ref[l] = cr
        cz_ref[l] = cz
        inv_ref[l] = inv
        v0_ref[l] = v0
        mine = own(v0)
        for g in range(2):
            for t in range(2):
                ret_ref[l, 2 * g + t] = mine[8 * g : 8 * g + 8, 128 * t : 128 * t + 128]
        return cz, s0 + folded(mine * (own(twice) * SCALE)), m0 + mine

    none = jnp.zeros((8, 128), F32)
    no_map = jnp.zeros((ROWS, WIDTH), F32)
    _, s0, m0 = lax.fori_loop(0, LAYERS, setup, (k_ref[0], none, no_map), unroll=8)

    def image(l, v_ref, fz_before):
        v = v_ref[l]
        fc = cc_ref[l] * (v - pltpu.roll(v, EXT_COLS - 1, axis=1))
        fr = cr_ref[l] * (v - pltpu.roll(v, EXT_ROWS - 1, axis=0))
        fz = cz_ref[l] * (v - v_ref[l + 1])
        result = (fc - pltpu.roll(fc, 1, axis=1)) + (fr - pltpu.roll(fr, 1, axis=0)) + (fz - fz_before)
        return v, result, fz

    def step(v_ref, out_ref, slot):
        def body(l, carry):
            fz_before, odd, even, total = carry
            v, result, fz = image(l, v_ref, fz_before)
            after = inv_ref[l] * result
            out_ref[l] = after
            mine = own(after)
            for g in range(2):
                for t in range(2):
                    ret_ref[l, 4 * slot + 2 * g + t] = mine[8 * g : 8 * g + 8, 128 * t : 128 * t + 128]
            got = own(result) * SCALE
            return fz, odd + folded(own(v) * got), even + folded(mine * got), total + mine

        start = (-(k_ref[0] * v_ref[0]), none, none, no_map)
        return lax.fori_loop(0, LAYERS, body, start, unroll=8)[1:]

    s1, s2, m1 = step(v0_ref, v1_ref, 1)
    s3, s4, m2 = step(v1_ref, v2_ref, 2)

    def last(l, carry):
        fz_before, odd = carry
        v, result, fz = image(l, v2_ref, fz_before)
        return fz, odd + folded(own(v) * (own(result) * SCALE))

    _, s5 = lax.fori_loop(0, LAYERS, last, (-(k_ref[0] * v2_ref[0]), none), unroll=16)

    sums = none
    for n, part in enumerate((s0, s1, s2, s3, s4, s5)):
        sums = jnp.where(sub == n, jnp.sum(part), sums)
    first = lax.broadcasted_iota(jnp.int32, (ROWS, 128), 1) % 8 < 4
    for f, total in enumerate((m0, m1, m2)):
        left, right = total[:, :128], total[:, 128:]
        square_ref[16 * f : 16 * f + 16, :] = jnp.where(first, left, pltpu.roll(right, 4, axis=1))
        square_ref[64 + 16 * f : 80 + 16 * f, :] = jnp.where(first, pltpu.roll(left, 124, axis=1), right)
    square_ref[48:56, :] = sums
    square_ref[56:64, :] = none
    square_ref[112:120, :] = none
    square_ref[120:128, :] = none
    turned = square_ref[...].T
    for j in range(LAYERS):
        msg_ref[j] = turned[8 * j : 8 * j + 8, :]


def tree(values):
    while len(values) > 1:
        values = [a + b for a, b in zip(values[::2], values[1::2])]
    return values[0]


def route_kernel(chosen_ref, recv_ref, msg_ref):
    lane = lax.broadcasted_iota(jnp.int32, (SLABS, 128), 1)
    shared = (lane >= 48) & (lane < 64)
    common = tree([recv_ref[j] for j in range(LAYERS)])
    chosen = chosen_ref[...]
    for q in range(4):
        strips = jnp.concatenate([recv_ref[:, q, :], recv_ref[:, 4 + q, :]], axis=0)
        sent = jnp.dot(chosen, strips, precision=lax.Precision.HIGHEST, preferred_element_type=F32)
        msg_ref[:, q, :] = jnp.where(shared, common[q : q + 1], sent)


def weights(s):
    level = jnp.where(s[0] > 2.0**60, 2.0**-60, jnp.where(s[0] < 2.0**-60, 2.0**60, 1.0))
    s0, s1, s2, s3, s4, s5 = [value * level for value in s]
    a0 = s0 / s1
    z1 = -a0
    n1 = s0 + z1 * (2.0 * s1 + z1 * s2)
    b0 = n1 / s0
    p0, p1 = 1.0 + b0, z1
    a1 = n1 / (p0 * p0 * s1 + p1 * (2.0 * p0 * s2 + p1 * s3))
    x0, x1 = a0 + a1 * p0, a1 * p1
    z1, z2 = z1 - a1 * p0, -(a1 * p1)
    n2 = s0 + z1 * (2.0 * s1 + z1 * s2) + z2 * (2.0 * (s2 + z1 * s3) + z2 * s4)
    b1 = n2 / n1
    p0, p1, p2 = 1.0 + b1 * p0, z1 + b1 * p1, z2
    energy = p0 * p0 * s1 + p1 * (2.0 * p0 * s2 + p1 * s3) + p2 * (2.0 * (p0 * s3 + p1 * s4) + p2 * s5)
    a2 = n2 / energy
    return x0 + a2 * p0, x1 + a2 * p1, a2 * p2


def solved(recv_ref):
    total = tree([recv_ref[s] for s in range(SLABS)])
    return weights([jnp.broadcast_to(total[:1, 48 + n : 49 + n], (8, 128)) for n in range(6)])


def combine_kernel(recv_ref, ret_ref, out_ref):
    w0, w1, w2 = solved(recv_ref)
    for l in range(LAYERS):
        for n in range(4):
            out_ref[l, n] = w0 * ret_ref[l, n] + w1 * ret_ref[l, 4 + n] + w2 * ret_ref[l, 8 + n]


def finish_kernel(rows_ref, recv_ref, back_ref, adjoint_ref, owned_ref):
    lane = lanes()
    sub = sublanes()
    for j in range(LAYERS):
        for n in range(4):
            col = WIDTH * j + 128 * (n % 2)
            adjoint_ref[0, 8 * (n // 2) : 8 * (n // 2) + 8, col : col + 128] = back_ref[j, n]
    w0, w1, w2 = solved(recv_ref)
    for k in range(OWNED):
        row = rows_ref[k]
        tile = jnp.zeros((8, 128), F32)
        for i in range(PER_TILE):
            half = recv_ref[PER_TILE * row + i]
            whole = jnp.concatenate([half, half], axis=0)
            strip = jnp.where(sub < 4, whole, pltpu.roll(whole, 64, axis=1))
            value = w0 * strip + w1 * pltpu.roll(strip, 112, axis=1) + w2 * pltpu.roll(strip, 96, axis=1)
            if i:
                value = pltpu.roll(value, 16 * i, axis=1)
            tile = jnp.where((lane >= 16 * i) & (lane < 16 * i + 16), value, tile)
        owned_ref[k] = tile


VMEM = pl.BlockSpec(memory_space=pltpu.VMEM)
SMEM = pl.BlockSpec(memory_space=pltpu.SMEM)


def shape(*dims):
    return jax.ShapeDtypeStruct(dims, F32)


def call(kernel, ins, outs, scratch=(), interpret=False):
    single = len(outs) == 1
    return pl.pallas_call(
        kernel,
        out_shape=outs[0] if single else tuple(outs),
        in_specs=ins,
        out_specs=VMEM if single else tuple(VMEM for _ in outs),
        scratch_shapes=list(scratch),
        compiler_params=pltpu.CompilerParams(vmem_limit_bytes=VMEM_LIMIT),
        interpret=interpret,
    )


def pack(turn, both, owner, interpret=False):
    outs = [shape(LAYERS, 9, 8, 128), jax.ShapeDtypeStruct(owner.shape, owner.dtype)]
    return call(pack_kernel, [SMEM] + [VMEM] * 2, outs, interpret=interpret)(turn, both, owner)


def halo(turn, recv, interpret=False):
    side = shape(2 * LAYERS + 1, 8, 128)
    return call(halo_kernel, [SMEM, VMEM], [side, side], interpret=interpret)(turn, recv)


def krylov(turn, recv, first, second, interpret=False):
    field = pltpu.VMEM((LAYERS + 1, EXT_ROWS, EXT_COLS), F32)
    face = pltpu.VMEM((LAYERS, EXT_ROWS, EXT_COLS), F32)
    return call(
        krylov_kernel,
        [SMEM] + [VMEM] * 3,
        [shape(LAYERS, 8, 128), shape(LAYERS, 12, 8, 128)],
        [field] * 4 + [face] * 4 + [pltpu.VMEM((128, 128), F32)],
        interpret=interpret,
    )(turn, recv, first, second)


def route(chosen, recv, interpret=False):
    return call(route_kernel, [VMEM] * 2, [shape(SLABS, 4, 128)], interpret=interpret)(chosen, recv)


def choices(table, index):
    owners = lax.dynamic_index_in_dim(table, lax.div(index, PER_TILE), 0, keepdims=False)
    owners = owners.reshape(TILE_COLS // 2, 2).T.reshape(1, TILE_COLS)
    return (owners == jnp.arange(SLABS, dtype=jnp.int32)[:, None]).astype(F32)


def combine(recv, ret, interpret=False):
    return call(combine_kernel, [VMEM] * 2, [shape(LAYERS, 4, 8, 128)], interpret=interpret)(recv, ret)


def finish(rows, recv, back, interpret=False):
    outs = [shape(1, ROWS, COLS), shape(OWNED, 8, 128)]
    return call(finish_kernel, [SMEM, VMEM, VMEM], outs, interpret=interpret)(rows, recv, back)


def owned_rows(tile_owner, index):
    held = jnp.any(tile_owner == index, axis=1)
    rank = jnp.cumsum(held.astype(jnp.int32)) - 1
    slot = jnp.arange(OWNED, dtype=jnp.int32)[:, None]
    row = jnp.arange(tile_owner.shape[0], dtype=jnp.int32)[None, :]
    return jnp.sum(jnp.where(held[None, :] & (rank[None, :] == slot), row, 0), axis=1)


def pairing(first):
    pairs = [(low, low + 1) for low in range(first, SLABS - 1, 2)]
    return pairs + [(high, low) for low, high in pairs]


def per_device(adjoint_source, conductivity, tile_owner):
    index = lax.axis_index("slab")
    turn = (index + 1).reshape(1)
    both = jnp.concatenate([conductivity, adjoint_source], axis=0)
    packed, table = pack(turn, both, tile_owner)
    recv = lax.all_to_all(packed, "layer", 0, 0, tiled=True)
    first, second = halo(turn, recv)
    first, table, index = lax.optimization_barrier((first, table, index))
    rows = owned_rows(table, index)
    chosen = choices(table, index)
    first = lax.ppermute(first, "slab", pairing(1))
    second = lax.ppermute(second, "slab", pairing(0))
    first, second, rows, chosen = lax.optimization_barrier((first, second, rows, chosen))
    msg, ret = krylov(turn, recv, first, second)
    strips = lax.all_to_all(msg, "layer", 0, 0, tiled=True)
    outgoing = route(chosen, strips)
    received = lax.all_to_all(outgoing, "slab", 0, 0, tiled=True)
    back = lax.all_to_all(combine(received, ret), "layer", 0, 0, tiled=True)
    return finish(rows, received, back)


def solution(mesh):
    placed = (P("layer", "slab", None), P("layer", "slab", None), P())
    return jax.shard_map(
        per_device,
        mesh=mesh,
        in_specs=placed,
        out_specs=(P("layer", "slab", None), P("slab", "layer", None)),
        check_vma=False,
    )
```
